256 devices in a mesh: seq: 16 (over z, x_hi), row: 8 (over y, core), col: 2 (over x_lo).
Axes of the slice: x: 4 (x_hi: 2, x_lo: 2; x = x_hi * 2 + x_lo), y: 4, z: 8, core: 2. Of those that a mesh axis runs over, the one named last changes fastest.
Arguments:
- projections: bfloat16 [3, 16384, 4096], P(None, 'seq', ('row', 'col')), may hold values from -6 to 6
- feat_filters: float32 [3, 7, 4096], P(None, None, ('row', 'col')), may hold values from -2 to 2
- long_filters: bfloat16 [256, 128], P(('row', 'col')), may hold values from -0.5 to 0.5
- out_weight: bfloat16 [4096, 8192], P('row', 'col'), may hold values from -0.09375 to 0.09375
- grad_output: bfloat16 [16384, 8192], P('seq', ('col', 'row')), may hold values from -6 to 6
Outputs:
- grad_projections: bfloat16 [3, 16384, 4096], P(None, 'seq', ('row', 'col'))
- grad_out_weight: float32 [4096, 8192], P('row', ('col', 'seq'))
- grad_long: float32 [256, 128], P(('row', 'col'))
- grad_feat: float32 [3, 7, 4096], P(None, None, ('row', 'col'))
The draws below stay inside these ranges and needn't reach their ends.
All inputs are finite; a program needn't handle non-finite values.
Results may differ from the reference program's by a relative error of at most 0.013.
Values may be sent and summed in bfloat16 or wider, within the bound.
A program may use at most 128 MiB of HBM per device.

```python
import math
import jax
import jax.numpy as jnp
from jax import lax

D = 8192
C = 4096
GS = 16
FL = 128
FW = 7
TOKENS = 16384
G = 256


def strengthened(values, own_key, source, target, blocks, factor):
    def block_of(position):
        return (jnp.arange(values.shape[position]) // (values.shape[position] // blocks)).reshape((-1,) + (1,) * (values.ndim - 1 - position))

    first = jax.random.permutation(own_key, blocks)[block_of(target)]
    other_side = (block_of(target) + blocks // 2) % blocks
    return jnp.where((block_of(source) == first) | (block_of(source) == other_side), factor * values, values)


def steps_of(stream_key, dims, shards, least, high):
    loudness = 1.0
    for axis_at, parts in shards:
        heights = jax.random.uniform(jax.random.fold_in(jax.random.fold_in(stream_key, 6), axis_at), (parts,), jnp.float32, least / len(shards), high / len(shards))
        loudness = loudness * jnp.repeat(jnp.exp(heights), dims[axis_at] // parts).reshape((-1,) + (1,) * (len(dims) - 1 - axis_at))
    return loudness


def gaussian(key, dims, scale, limit, shards=(), held_as=jnp.bfloat16):
    drawn = scale * jax.random.normal(key, dims, jnp.float32)
    if shards:
        drawn = drawn * steps_of(key, dims, shards, -0.22, 0.18)
    return jnp.clip(drawn, -limit, limit).astype(held_as)


def heavy_noise(key, extent, width, most, cuts, heavy, kind=jnp.bfloat16):
    entries = width * jax.random.normal(key, extent, jnp.float32)
    if cuts:
        entries = entries * steps_of(key, extent, cuts, -0.22, 0.18)
    return jnp.clip(strengthened(entries, jax.random.fold_in(key, 3), *heavy), -most, most).astype(kind)


def setup_inputs(seed: int = 0) -> dict:
    key_list = jax.random.split(jax.random.key(seed), 6)
    return {
        "projections": gaussian(key_list[0], (3, TOKENS, C), 1.0, 6.0, ((1, 16), (2, 16))),
        "feat_filters": gaussian(key_list[1], (3, FW, C), FW ** -0.5, 2.0, ((2, 16),), jnp.float32),
        "long_filters": gaussian(key_list[2], (G, FL), FL ** -0.5, 0.5, ((0, 16),)),
        "out_weight": gaussian(key_list[3], (C, D), C ** -0.5, 0.09375, ((0, 8), (1, 2))),
        "grad_output": heavy_noise(key_list[4], (TOKENS, D), 1.0, 6.0, ((0, 16), (1, 16)), (0, 1, 16, 2.0)),
    }


def causal_taps(signal, tap_table):
    tap_count = tap_table.shape[0]
    length_all = signal.shape[0]
    padded = jnp.concatenate([jnp.zeros((tap_count - 1, signal.shape[1]), jnp.float32), signal], 0)

    def add_tap(tap_idx, total_acc):
        window = lax.dynamic_slice_in_dim(padded, (tap_count - 1 - tap_idx).astype(jnp.int32), length_all, 0)
        return total_acc + lax.dynamic_index_in_dim(tap_table, tap_idx.astype(jnp.int32), 0, keepdims=False) * window
    return lax.fori_loop(jnp.int32(0), jnp.int32(tap_count), add_tap, jnp.zeros(signal.shape, jnp.float32))

def future_taps(signal, tap_table):
    tap_count = tap_table.shape[0]
    length_all = signal.shape[0]
    padded = jnp.concatenate([signal, jnp.zeros((tap_count - 1, signal.shape[1]), jnp.float32)], 0)

    def add_tap(tap_idx, total_acc):
        window = lax.dynamic_slice_in_dim(padded, tap_idx.astype(jnp.int32), length_all, 0)
        return total_acc + lax.dynamic_index_in_dim(tap_table, tap_idx.astype(jnp.int32), 0, keepdims=False) * window
    return lax.fori_loop(jnp.int32(0), jnp.int32(tap_count), add_tap, jnp.zeros(signal.shape, jnp.float32))

def reference(projections, feat_filters, long_filters, out_weight, grad_output):
    grad_scale = 1.0 / math.sqrt(TOKENS)
    inputs = projections.astype(jnp.float32)
    query_feat = causal_taps(inputs[0], feat_filters[0])
    key_feat = causal_taps(inputs[1], feat_filters[1])
    value_feat = causal_taps(inputs[2], feat_filters[2])
    kv_product = (key_feat * value_feat).astype(jnp.bfloat16)
    tap_table = jnp.repeat(long_filters.astype(jnp.float32), GS, axis=0).T
    kv_float = kv_product.astype(jnp.float32)
    conv_out = causal_taps(kv_float, tap_table)
    mixer_out = (query_feat * conv_out).astype(jnp.bfloat16)
    grad_mix = lax.dot_general(grad_output, out_weight, (((1,), (1,)), ((), ())), preferred_element_type=jnp.float32).astype(jnp.bfloat16)
    grad_weight = lax.dot_general(mixer_out, grad_output, (((0,), (0,)), ((), ())), preferred_element_type=jnp.float32) * grad_scale
    mix_float = grad_mix.astype(jnp.float32)
    grad_conv = (mix_float * query_feat).astype(jnp.bfloat16)
    grad_query = (mix_float * conv_out).astype(jnp.bfloat16)
    conv_float = grad_conv.astype(jnp.float32)
    kv_padded = jnp.concatenate([jnp.zeros((FL - 1, C), jnp.float32), kv_float], 0)

    def lag_sum(lag_idx):
        window = lax.dynamic_slice_in_dim(kv_padded, (FL - 1 - lag_idx).astype(jnp.int32), TOKENS, 0)
        return lax.optimization_barrier(jnp.sum((conv_float * window).reshape(TOKENS, G, GS), axis=(0, 2)))
    grad_long = lax.map(lag_sum, jnp.arange(FL, dtype=jnp.int32)).T * grad_scale
    grad_kv = future_taps(conv_float, tap_table)
    grad_key = (grad_kv * value_feat).astype(jnp.bfloat16)
    grad_value = (grad_kv * key_feat).astype(jnp.bfloat16)
    stream_grads = [grad_query, grad_key, grad_value]
    grad_list = []
    feat_list = []
    for stream in range(3):
        grad_float = stream_grads[stream].astype(jnp.float32)
        grad_list.append(future_taps(grad_float, feat_filters[stream]).astype(jnp.bfloat16))
        padded = jnp.concatenate([jnp.zeros((FW - 1, C), jnp.float32), inputs[stream]], 0)
        per_tap = []
        for tap_idx in range(FW):
            window = padded[FW - 1 - tap_idx:FW - 1 - tap_idx + TOKENS]
            per_tap.append(lax.optimization_barrier(jnp.sum(grad_float * window, axis=0)))
        feat_list.append(jnp.stack(per_tap, 0))
    grad_projections = jnp.stack(grad_list, 0)
    grad_feat = jnp.stack(feat_list, 0) * grad_scale
    return (grad_projections, grad_weight, grad_long, grad_feat)
```

```python
import functools
import math

import jax
import jax.numpy as jnp
from jax import lax
from jax.experimental import pallas as pl
from jax.experimental.pallas import tpu as pltpu
from jax.sharding import PartitionSpec as P

MESH = pl.DeviceIdType.MESH
F32 = jnp.float32
BF16 = jnp.bfloat16
NN = (((1,), (0,)), ((), ()))
NT = (((1,), (1,)), ((), ()))
TN = (((0,), (0,)), ((), ()))
Z = 8
Y = 4
TOK = 1024
CH = 256
LANES = 128
BLOCKS = TOK // LANES
GROUPS = 16
GS = 16
TAPS = 7
PARTS = 4
RIM = 16
ORDER = (0, 2, 1, 3)
UNITS = 2 * PARTS
COPIES = 160


def dot(a, b, dims):
    return lax.dot_general(a, b, dims, preferred_element_type=F32)


def kernel(
    grad_scale,
    proj,
    ff,
    lf,
    w_hbm,
    go_hbm,
    gp_out,
    gw_out,
    gl_out,
    gf_out,
    projx,
    feat,
    kvx,
    conv,
    mix,
    toep,
    wv,
    gath,
    pm,
    part,
    rsbuf,
    gwacc,
    xs,
    xr,
    gms,
    gmr,
    gcx,
    gback,
    gtok,
    rim_in,
    rim_out,
    rim_back,
    red,
    redx,
    redz,
    ssem,
    rsem,
    lsem,
):
    s = lax.axis_index("seq")
    r = lax.axis_index("row")
    q = lax.axis_index("col")
    seqs = 2 * Z
    z, xh = s // 2, s % 2
    y, core = r // 2, r % 2

    def at_z(k):
        return (((z + k) % Z) * 2 + xh, r, q)

    def at_y(k):
        return (s, ((y + k) % Y) * 2 + core, q)

    def row_y(k, c):
        return ((y + k) % Y) * 2 + c

    sibling = (s, y * 2 + 1 - core, q)
    across = (z * 2 + 1 - xh, r, q)
    column = (s, r, 1 - q)
    after = ((s + 1) % seqs, r, q)
    behind = ((s + seqs - 1) % seqs, r, q)
    diagonal = (((z + 2 * xh - 1 + Z) % Z) * 2 + 1 - xh, r, q)

    used = [0]
    sent = []

    def push(src, dst, device):
        idx = used[0]
        used[0] += 1
        copy = pltpu.make_async_remote_copy(
            src_ref=src,
            dst_ref=dst,
            send_sem=ssem.at[idx],
            recv_sem=rsem.at[idx],
            device_id=device,
            device_id_type=MESH,
        )
        copy.start()
        sent.append(copy)
        return idx

    def arrived(idx, ref):
        pltpu.make_async_remote_copy(
            src_ref=ref,
            dst_ref=ref,
            send_sem=ssem.at[idx],
            recv_sem=rsem.at[idx],
            device_id=sibling,
            device_id_type=MESH,
        ).wait_recv()

    w_loads = []
    for p in range(PARTS):
        for blk in range(2 * Y):
            copy = pltpu.make_async_copy(
                w_hbm.at[:, pl.ds(512 * blk + LANES * ORDER[p], LANES)],
                wv.at[p, :, pl.ds(LANES * blk, LANES)],
                lsem.at[p * 9 + blk],
            )
            copy.start()
            w_loads.append(copy)
    own_loads = []
    for p in range(PARTS):
        copy = pltpu.make_async_copy(
            go_hbm.at[:, pl.ds(LANES * ORDER[p], LANES)], gath.at[p, r], lsem.at[p * 9 + 8]
        )
        copy.start()
        own_loads.append(copy)

    barrier = pltpu.get_barrier_semaphore()
    partners = [at_z(k) for k in range(1, Z)] + [at_y(1), at_y(-1 + Y), sibling, across, column, diagonal]
    for device in partners:
        pl.semaphore_signal(barrier, inc=1, device_id=device, device_id_type=MESH)
    pl.semaphore_wait(barrier, len(partners))

    ids = {}

    def gather_direct(p):
        src = go_hbm.at[:, pl.ds(LANES * ORDER[p], LANES)]
        ids[p, 0] = push(src, gath.at[p, r], at_y(1))
        ids[p, 1] = push(src, gath.at[p, r], at_y(Y - 1))
        ids[p, 2] = push(src, gath.at[p, r], sibling)

    half = pl.ds(0, TOK // 2), pl.ds(TOK // 2, TOK // 2)

    def gather_forward(p):
        low, high = row_y(Y - 1, core), row_y(1, core)
        arrived(ids[p, 0], gath.at[p, low])
        ids[p, 3] = push(gath.at[p, low, half[0]], gath.at[p, low, half[0]], at_y(1))
        ids[p, 5] = push(gath.at[p, low], gath.at[p, low], sibling)
        arrived(ids[p, 1], gath.at[p, high])
        ids[p, 4] = push(gath.at[p, high, half[1]], gath.at[p, high, half[1]], at_y(Y - 1))
        ids[p, 6] = push(gath.at[p, high], gath.at[p, high], sibling)

    def gather_finish(p):
        far = row_y(2, core)
        arrived(ids[p, 3], gath.at[p, far, half[0]])
        arrived(ids[p, 4], gath.at[p, far, half[1]])
        ids[p, 7] = push(gath.at[p, far], gath.at[p, far], sibling)
        own_loads[p].wait()
        for idx, k in ((2, 0), (5, Y - 1), (6, 1), (7, 2)):
            arrived(ids[p, idx], gath.at[p, row_y(k, 1 - core)])

    gather_direct(0)
    rim_id = push(proj.at[:, pl.ds(TOK - RIM, RIM), :], rim_in, after)
    gather_direct(1)

    taps32 = lf[...].astype(F32)
    base = jnp.broadcast_to(taps32[:, None, :], (GROUPS, 8, LANES)).reshape(GROUPS * 8, LANES)
    sub = lax.broadcasted_iota(jnp.int32, (GROUPS * 8, LANES), 0) % 8
    for bit in (1, 2, 4):
        base = jnp.where((sub // bit) % 2 == 1, pltpu.roll(base, bit, 1), base)
    lane3 = lax.broadcasted_iota(jnp.int32, (GROUPS, 16, LANES), 2)
    sub3 = lax.broadcasted_iota(jnp.int32, (GROUPS, 16, LANES), 1)
    for a in range(LANES // 16):
        low = pltpu.roll(base, 16 * a, 1) if a else base
        high = pltpu.roll(base, 16 * a + 8, 1)
        both = jnp.concatenate(
            [low.reshape(GROUPS, 8, LANES), high.reshape(GROUPS, 8, LANES)], axis=1
        )
        later = lane3 < sub3 + 16 * a
        toep[:, pl.ds(16 * a, 16), :] = jnp.where(later, both, 0.0).astype(BF16)
        toep[:, pl.ds(LANES + 16 * a, 16), :] = jnp.where(later, 0.0, both).astype(BF16)

    def widen(b, carry):
        rows = pl.ds(pl.multiple_of(b * LANES, LANES), LANES)
        dest = pl.ds(pl.multiple_of(b * LANES + RIM, RIM), LANES)
        for a in range(3):
            block = proj[a, rows, :].astype(F32)
            for h in range(2):
                projx[a, h, dest, :] = block[:, LANES * h : LANES * h + LANES]
        return carry

    lax.fori_loop(0, BLOCKS, widen, 0)

    def featurize(b):
        start = b * LANES + RIM
        cols = pl.ds(b * LANES if isinstance(b, int) else pl.multiple_of(b * LANES, LANES), LANES)
        for h in range(2):
            chans = pl.ds(LANES * h, LANES)
            turned = []
            for a in range(3):
                total = ff[a, pl.ds(0, 1), chans] * projx[a, h, pl.ds(start, LANES), :]
                for i in range(1, TAPS):
                    total = total + ff[a, pl.ds(i, 1), chans] * projx[a, h, pl.ds(start - i, LANES), :]
                total = total.T
                feat[a, chans, cols] = total
                turned.append(total)
            product = (turned[1] * turned[2]).astype(BF16)
            ahead = b * LANES + LANES
            kvx[chans, pl.ds(ahead if isinstance(b, int) else pl.multiple_of(ahead, LANES), LANES)] = product

    featurize(BLOCKS - 1)
    hist_id = push(kvx.at[:, pl.ds(TOK, LANES)], kvx.at[:, pl.ds(0, LANES)], after)

    def feat_loop(b, carry):
        featurize(b)
        return carry

    lax.fori_loop(1, BLOCKS - 1, feat_loop, 0)
    arrived(rim_id, rim_in)
    for a in range(3):
        before = jnp.where(s == 0, 0.0, rim_in[a].astype(F32))
        for h in range(2):
            projx[a, h, pl.ds(0, RIM), :] = before[:, LANES * h : LANES * h + LANES]
    featurize(0)

    gather_forward(0)
    gather_direct(2)

    arrived(hist_id, kvx.at[:, pl.ds(0, LANES)])
    past = kvx[:, pl.ds(0, LANES)]
    kvx[:, pl.ds(0, LANES)] = jnp.where(s == 0, jnp.zeros_like(past), past)

    def stacked(ref, rows, first):
        return jnp.concatenate(
            [ref[rows, pl.ds(LANES * (b + first), LANES)] for b in range(BLOCKS)], axis=0
        )

    def convolve(g, carry):
        rows = pl.ds(pl.multiple_of(g * GS, GS), GS)
        windows = jnp.concatenate([stacked(kvx, rows, 0), stacked(kvx, rows, 1)], axis=1)
        result = dot(windows, toep[g], NN)
        for b in range(BLOCKS):
            cols = pl.ds(LANES * b, LANES)
            piece = result[GS * b : GS * b + GS]
            conv[rows, cols] = piece
            mix[q, rows, cols] = (feat[0, rows, cols] * piece).astype(BF16)
        return carry

    mix_ids = []
    for h in range(2):
        lax.fori_loop(h * GROUPS // 2, (h + 1) * GROUPS // 2, convolve, 0)
        chans = pl.ds(LANES * h, LANES)
        mix_ids.append((push(mix.at[q, chans], mix.at[q, chans], column), chans))

    rs = {}
    top, bottom = pl.ds(0, CH // 2), pl.ds(CH // 2, CH // 2)

    def side(n):
        return q if n % 2 == 0 else 1 - q

    def partial_weight(n):
        p, hh = n // 2, side(n)

        def pair(i, carry):
            rhs = jnp.concatenate([gath[p, 2 * i], gath[p, 2 * i + 1]], axis=1)
            result = dot(mix[hh], rhs, NN).astype(BF16)
            part[n, 2 * i] = result[:, :LANES]
            part[n, 2 * i + 1] = result[:, LANES:]
            return carry

        lax.fori_loop(0, Y, pair, 0)

    def hop(n, k):
        ahead, back = (z + k) % Z, (z - k + Z) % Z
        if k == 4:
            rs[n, 0, 0] = push(part.at[n, ahead, top], rsbuf.at[n, 0, 0, top], at_z(1))
            rs[n, 1, 0] = push(part.at[n, ahead, bottom], rsbuf.at[n, 1, 0, bottom], at_z(Z - 1))
            return
        step = 3 - k
        for way, dest, span, there in ((0, ahead, top, 1), (1, back, bottom, Z - 1)):
            rows = span if k == 3 else pl.ds(0, CH)
            arrived(rs[n, way, step], rsbuf.at[n, way, step, rows])
            part[n, dest, rows] = (
                part[n, dest, rows].astype(F32) + rsbuf[n, way, step, rows].astype(F32)
            ).astype(BF16)
            rs[n, way, step + 1] = push(part.at[n, dest], rsbuf.at[n, way, step + 1], at_z(there))

    def final_sum(n):
        for way in range(2):
            arrived(rs[n, way, 3], rsbuf.at[n, way, 3])
        gwacc[n // 2, side(n)] = (
            part[n, z].astype(F32) + rsbuf[n, 0, 3].astype(F32) + rsbuf[n, 1, 3].astype(F32)
        )

    xids = []

    def exchange(pair):
        xs[pair] = gwacc[2 * pair + 1 - xh].astype(BF16)
        xids.append(push(xs.at[pair], xr.at[pair], across))

    def tick(t):
        if t < UNITS:
            partial_weight(t)
            hop(t, 4)
        for lag in (1, 2, 3):
            if 0 <= t - lag < UNITS:
                hop(t - lag, 4 - lag)
        if 0 <= t - 4 < UNITS:
            final_sum(t - 4)
            if t - 4 == 3:
                exchange(0)
            if t - 4 == 7:
                exchange(1)

    def mix_tile(p, hh, j):
        trows = pl.ds(pl.multiple_of(j * CH, CH), CH)
        crows = pl.ds(pl.multiple_of(hh * CH, CH), CH)
        rhs = jnp.concatenate([gath[p, i, trows, :] for i in range(2 * Y)], axis=1)
        return dot(wv[p, crows, :], rhs, NT)

    def partial_mix(p):
        def tile(j, carry):
            for hh in range(2):
                value = mix_tile(p, hh, j)
                if p == 0:
                    pm[j, hh] = value
                else:
                    pm[j, hh] += value
            return carry

        lax.fori_loop(0, TOK // CH, tile, 0)

    gather_forward(1)
    gather_direct(3)
    for copy in w_loads:
        copy.wait()
    for p in range(PARTS - 1):
        gather_finish(p)
        tick(2 * p)
        gather_forward(p + 2) if p + 2 < PARTS else None
        partial_mix(p)
        if p == 0:
            for idx, chans in mix_ids:
                arrived(idx, mix.at[1 - q, chans])
        tick(2 * p + 1)

    last = PARTS - 1
    gather_finish(last)
    gm_ids = []
    for j in range(TOK // CH):
        gms[j] = (pm[j, 1 - q] + mix_tile(last, 1 - q, j)).astype(BF16)
        gm_ids.append(push(gms.at[j], gmr.at[j], column))
    tick(6)
    for j in range(TOK // CH):
        pm[j, q] += mix_tile(last, q, j)
    tick(7)

    for j in range(TOK // CH):
        arrived(gm_ids[j], gmr.at[j])
        cols = pl.ds(CH * j, CH)
        cot = (pm[j, q] + gmr[j].astype(F32)).astype(BF16).astype(F32)
        gcx[:, cols] = (cot * feat[0, :, cols]).astype(BF16)
        gback[0, :, cols] = (cot * conv[:, cols]).astype(BF16).astype(F32)
        if j == 0:
            future_id = push(gcx.at[:, pl.ds(0, LANES)], gcx.at[:, pl.ds(TOK, LANES)], behind)
    tick(8)

    lane = lax.broadcasted_iota(jnp.int32, (LANES, LANES), 1)
    row = lax.broadcasted_iota(jnp.int32, (LANES, LANES), 0)

    def lags(g, carry):
        rows = pl.ds(pl.multiple_of(g * GS, GS), GS)
        cot = stacked(gcx, rows, 0)
        upper = dot(stacked(kvx, rows, 0), cot, TN)
        lower = dot(stacked(kvx, rows, 1), cot, TN)
        table = jnp.where(lane < row, upper, lower)
        height = LANES // 2
        while height >= 8:
            table = table[:height] + pltpu.roll(table[height:], LANES - height, 1)
            height //= 2
        redx[1, pl.ds(pl.multiple_of(g * 8, 8), 8), :] = table
        return carry

    lax.fori_loop(0, GROUPS, lags, 0)
    table = redx[1]
    for bit in (1, 2, 4):
        table = jnp.where((sub // bit) % 2 == 1, pltpu.roll(table, LANES - bit, 1), table)
    red[pl.ds(0, GROUPS), :] = jnp.sum(table.reshape(GROUPS, 8, LANES), axis=1)
    tick(9)

    arrived(future_id, gcx.at[:, pl.ds(TOK, LANES)])
    coming = gcx[:, pl.ds(TOK, LANES)]
    gcx[:, pl.ds(TOK, LANES)] = jnp.where(s == seqs - 1, jnp.zeros_like(coming), coming)

    def deconvolve(g, carry):
        rows = pl.ds(pl.multiple_of(g * GS, GS), GS)
        windows = jnp.concatenate([stacked(gcx, rows, 0), stacked(gcx, rows, 1)], axis=1)
        band = jnp.concatenate([toep[g, pl.ds(LANES, LANES), :], toep[g, pl.ds(0, LANES), :]], axis=1)
        result = dot(windows, band, NT)
        for b in range(BLOCKS):
            cols = pl.ds(LANES * b, LANES)
            piece = result[GS * b : GS * b + GS]
            gback[1, rows, cols] = (piece * feat[2, rows, cols]).astype(BF16).astype(F32)
            gback[2, rows, cols] = (piece * feat[1, rows, cols]).astype(BF16).astype(F32)
        return carry

    lax.fori_loop(0, GROUPS, deconvolve, 0)
    tick(10)

    def turn(b, carry):
        cols = pl.ds(pl.multiple_of(b * LANES, LANES), LANES)
        for a in range(3):
            for h in range(2):
                gtok[a, h, cols, :] = gback[a, pl.ds(LANES * h, LANES), cols].T
        return carry

    lax.fori_loop(0, BLOCKS, turn, 0)
    for a in range(3):
        for h in range(2):
            rim_out[a, :, pl.ds(LANES * h, LANES)] = gtok[a, h, pl.ds(0, RIM), :].astype(BF16)
    back_id = push(rim_out, rim_back, behind)
    tick(11)

    span = 64

    def tap_sums(a, h):
        def body(b, sums):
            start = pl.multiple_of(b * span, span)
            grad = gtok[a, h, pl.ds(start, span), :]
            out = []
            for i in range(TAPS):
                value = grad * projx[a, h, pl.ds(start + RIM - i, span), :]
                out.append(sums[i] + jnp.sum(value.reshape(span // 8, 8, LANES), axis=0))
            return tuple(out)

        sums = lax.fori_loop(0, TOK // span, body, tuple(jnp.zeros((8, LANES), F32) for _ in range(TAPS)))
        rows = [jnp.sum(x, axis=0, keepdims=True) for x in sums] + [jnp.zeros((1, LANES), F32)]
        red[pl.ds(GROUPS + 8 * (2 * a + h), 8), :] = jnp.concatenate(rows, axis=0)

    for a in range(3):
        for h in range(2):
            tap_sums(a, h)
    width = GROUPS + 48
    red_id = push(red, redx.at[0, pl.ds(0, width), :], across)

    def taps_back(a, h, first, count):
        chans = pl.ds(LANES * h, LANES)

        def body(b, carry):
            start = pl.multiple_of(b * span, span)
            total = ff[a, pl.ds(0, 1), chans] * gtok[a, h, pl.ds(start, span), :]
            for i in range(1, TAPS):
                total = total + ff[a, pl.ds(i, 1), chans] * gtok[a, h, pl.ds(start + i, span), :]
            gp_out[a, pl.ds(start, span), chans] = total.astype(BF16)
            return carry

        lax.fori_loop(first, first + count, body, 0)

    for h in range(2):
        taps_back(0, h, 0, TOK // span - 1)
    arrived(red_id, redx.at[0, pl.ds(0, width), :])
    redz[0] = red[...] + redx[0, pl.ds(0, width), :]
    z_ids = [push(redz.at[0], redz.at[k], at_z(k)) for k in range(1, Z)]
    for a in (1, 2):
        for h in range(2):
            taps_back(a, h, 0, TOK // span - 1)
    arrived(back_id, rim_back)
    for a in range(3):
        rest = jnp.where(s == seqs - 1, 0.0, rim_back[a].astype(F32))
        for h in range(2):
            gtok[a, h, pl.ds(TOK, RIM), :] = rest[:, LANES * h : LANES * h + LANES]
            taps_back(a, h, TOK // span - 1, 1)

    for pair in range(2):
        arrived(xids[pair], xr.at[pair])
        for hh in range(2):
            gw_out[pl.ds(CH * hh, CH), pl.ds(LANES * pair, LANES)] = (
                gwacc[2 * pair + xh, hh] + xr[pair, hh].astype(F32)
            ) * grad_scale

    for k in range(1, Z):
        arrived(z_ids[k - 1], redz.at[k])
    total = redz[0]
    for k in range(1, Z):
        total = total + redz[k]
    total = total * grad_scale
    gl_out[...] = total[:GROUPS]
    for a in range(3):
        for h in range(2):
            at = GROUPS + 8 * (2 * a + h)
            gf_out[a, :, pl.ds(LANES * h, LANES)] = total[at : at + TAPS]
    for copy in sent:
        copy.wait_send()


def on_device(projections, feat_filters, long_filters, out_weight, grad_output):
    grad_scale = 1.0 / math.sqrt(TOK * 2 * Z)
    vmem = pl.BlockSpec(memory_space=pltpu.VMEM)
    anywhere = pl.BlockSpec(memory_space=pl.ANY)
    return pl.pallas_call(
        functools.partial(kernel, grad_scale),
        out_shape=(
            jax.ShapeDtypeStruct((3, TOK, CH), BF16),
            jax.ShapeDtypeStruct((2 * CH, 2 * LANES), F32),
            jax.ShapeDtypeStruct((GROUPS, LANES), F32),
            jax.ShapeDtypeStruct((3, TAPS, CH), F32),
        ),
        in_specs=[vmem, vmem, vmem, anywhere, anywhere],
        out_specs=(vmem, vmem, vmem, vmem),
        scratch_shapes=[
            pltpu.VMEM((3, 2, TOK + RIM, LANES), F32),
            pltpu.VMEM((3, CH, TOK), F32),
            pltpu.VMEM((CH, TOK + LANES), BF16),
            pltpu.VMEM((CH, TOK), F32),
            pltpu.VMEM((2, CH, TOK), BF16),
            pltpu.VMEM((GROUPS, 2 * LANES, LANES), BF16),
            pltpu.VMEM((PARTS, 2 * CH, 2 * Y * LANES), BF16),
            pltpu.VMEM((PARTS, 2 * Y, TOK, LANES), BF16),
            pltpu.VMEM((TOK // CH, 2, CH, CH), F32),
            pltpu.VMEM((UNITS, Z, CH, LANES), BF16),
            pltpu.VMEM((UNITS, 2, 4, CH, LANES), BF16),
            pltpu.VMEM((PARTS, 2, CH, LANES), F32),
            pltpu.VMEM((2, 2, CH, LANES), BF16),
            pltpu.VMEM((2, 2, CH, LANES), BF16),
            pltpu.VMEM((TOK // CH, CH, CH), BF16),
            pltpu.VMEM((TOK // CH, CH, CH), BF16),
            pltpu.VMEM((CH, TOK + LANES), BF16),
            pltpu.VMEM((3, CH, TOK), F32),
            pltpu.VMEM((3, 2, TOK + RIM, LANES), F32),
            pltpu.VMEM((3, RIM, CH), BF16),
            pltpu.VMEM((3, RIM, CH), BF16),
            pltpu.VMEM((3, RIM, CH), BF16),
            pltpu.VMEM((GROUPS + 48, LANES), F32),
            pltpu.VMEM((2, 8 * GROUPS, LANES), F32),
            pltpu.VMEM((Z, GROUPS + 48, LANES), F32),
            pltpu.SemaphoreType.DMA((COPIES,)),
            pltpu.SemaphoreType.DMA((COPIES,)),
            pltpu.SemaphoreType.DMA((9 * PARTS,)),
        ],
        compiler_params=pltpu.CompilerParams(
            collective_id=0, has_side_effects=True, vmem_limit_bytes=60 * 1024 * 1024
        ),
        cost_estimate=pl.CostEstimate(
            flops=9_000_000_000, bytes_accessed=20_000_000, transcendentals=0
        ),
    )(projections, feat_filters, long_filters, out_weight, grad_output)


def solution(mesh):
    return jax.shard_map(
        on_device,
        mesh=mesh,
        in_specs=(
            P(None, "seq", ("row", "col")),
            P(None, None, ("row", "col")),
            P(("row", "col"), None),
            P("row", "col"),
            P("seq", ("col", "row")),
        ),
        out_specs=(
            P(None, "seq", ("row", "col")),
            P("row", ("col", "seq")),
            P(("row", "col"), None),
            P(None, None, ("row", "col")),
        ),
        check_vma=False,
    )
```

```python
import functools
import math

import jax
import jax.numpy as jnp
from jax import lax
from jax.experimental import pallas as pl
from jax.experimental.pallas import tpu as pltpu
from jax.sharding import PartitionSpec as P

MESH = pl.DeviceIdType.MESH
F32 = jnp.float32
BF16 = jnp.bfloat16
NN = (((1,), (0,)), ((), ()))
NT = (((1,), (1,)), ((), ()))
TN = (((0,), (0,)), ((), ()))
Z = 8
Y = 4
TOK = 1024
CH = 256
LANES = 128
BLOCKS = TOK // LANES
GROUPS = 16
GS = 16
TAPS = 7
PARTS = 4
RIM = 16
ORDER = (0, 2, 1, 3)
UNITS = 2 * PARTS
COPIES = 176
PIECES = ((0, 0), (0, 1), (1, 0), (1, 1), (2, 0), (3, 0), (2, 1), (3, 1))
HALF = TOK // 2
UNROLL = 4


def dot(a, b, dims):
    return lax.dot_general(a, b, dims, preferred_element_type=F32)


def kernel(
    grad_scale,
    proj_hbm,
    ff,
    lf,
    w_hbm,
    go_hbm,
    gp_out,
    gw_out,
    gl_out,
    gf_out,
    proj,
    projx,
    feat,
    kvx,
    conv,
    mix,
    toep,
    wv,
    gath,
    pm,
    part,
    rsbuf,
    gwacc,
    xs,
    xr,
    gms,
    gmr,
    gcx,
    gback,
    gtok,
    rim_in,
    rim_out,
    rim_back,
    lagt,
    red,
    redr,
    redt,
    redo,
    ssem,
    rsem,
    lsem,
):
    s = lax.axis_index("seq")
    r = lax.axis_index("row")
    q = lax.axis_index("col")
    seqs = 2 * Z
    z, xh = s // 2, s % 2
    y, core = r // 2, r % 2

    def at_z(k):
        return (((z + k) % Z) * 2 + xh, r, q)

    def at_s(k):
        return ((s + k) % seqs, r, q)

    def at_y(k):
        return (s, ((y + k) % Y) * 2 + core, q)

    def row_y(k, c):
        return ((y + k) % Y) * 2 + c

    sibling = (s, y * 2 + 1 - core, q)
    across = (z * 2 + 1 - xh, r, q)
    column = (s, r, 1 - q)
    after = ((s + 1) % seqs, r, q)
    behind = ((s + seqs - 1) % seqs, r, q)

    used = [0]
    sent = []

    def push(src, dst, device):
        idx = used[0]
        used[0] += 1
        copy = pltpu.make_async_remote_copy(
            src_ref=src,
            dst_ref=dst,
            send_sem=ssem.at[idx],
            recv_sem=rsem.at[idx],
            device_id=device,
            device_id_type=MESH,
        )
        copy.start()
        sent.append(copy)
        return idx

    def arrived(idx, ref):
        pltpu.make_async_remote_copy(
            src_ref=ref,
            dst_ref=ref,
            send_sem=ssem.at[idx],
            recv_sem=rsem.at[idx],
            device_id=sibling,
            device_id_type=MESH,
        ).wait_recv()

    barrier = pltpu.get_barrier_semaphore()
    partners = [at_s(k) for k in range(1, seqs)] + [at_y(1), at_y(Y - 1), sibling, column]
    for device in partners:
        pl.semaphore_signal(barrier, inc=1, device_id=device, device_id_type=MESH)
    proj_load = pltpu.make_async_copy(proj_hbm, proj, lsem.at[9 * PARTS])
    proj_load.start()
    own_loads = []
    for p in range(PARTS):
        copy = pltpu.make_async_copy(
            go_hbm.at[:, pl.ds(LANES * ORDER[p], LANES)], gath.at[p, r], lsem.at[p * 9 + 8]
        )
        copy.start()
        own_loads.append(copy)

    taps32 = lf[...].astype(F32)
    base = jnp.broadcast_to(taps32[:, None, :], (GROUPS, 8, LANES)).reshape(GROUPS * 8, LANES)
    sub = lax.broadcasted_iota(jnp.int32, (GROUPS * 8, LANES), 0) % 8
    for bit in (1, 2, 4):
        base = jnp.where((sub // bit) % 2 == 1, pltpu.roll(base, bit, 1), base)
    lane3 = lax.broadcasted_iota(jnp.int32, (GROUPS, 16, LANES), 2)
    sub3 = lax.broadcasted_iota(jnp.int32, (GROUPS, 16, LANES), 1)
    for a in range(LANES // 16):
        low = pltpu.roll(base, 16 * a, 1) if a else base
        high = pltpu.roll(base, 16 * a + 8, 1)
        both = jnp.concatenate(
            [low.reshape(GROUPS, 8, LANES), high.reshape(GROUPS, 8, LANES)], axis=1
        )
        later = lane3 < sub3 + 16 * a
        toep[:, pl.ds(16 * a, 16), :] = jnp.where(later, both, 0.0).astype(BF16)
        toep[:, pl.ds(LANES + 16 * a, 16), :] = jnp.where(later, 0.0, both).astype(BF16)

    pl.semaphore_wait(barrier, len(partners))

    ids = {}

    def tokens(hf, quarter=None):
        if quarter is None:
            return pl.ds(HALF * hf, HALF)
        return pl.ds(HALF * hf + HALF // 2 * quarter, HALF // 2)

    def direct(i):
        p, hf = PIECES[i]
        src = go_hbm.at[tokens(hf), pl.ds(LANES * ORDER[p], LANES)]
        dst = gath.at[p, r, tokens(hf)]
        ids[i, 0] = push(src, dst, at_y(1))
        ids[i, 1] = push(src, dst, at_y(Y - 1))
        ids[i, 2] = push(src, dst, sibling)

    def forward(i):
        p, hf = PIECES[i]
        for way, k, there in ((0, Y - 1, 1), (1, 1, Y - 1)):
            slot = row_y(k, core)
            arrived(ids[i, way], gath.at[p, slot, tokens(hf)])
            src = gath.at[p, slot, tokens(hf, way)]
            ids[i, 3 + way] = push(src, src, at_y(there))
            src = gath.at[p, slot, tokens(hf)]
            ids[i, 5 + way] = push(src, src, sibling)

    def finish(i):
        p, hf = PIECES[i]
        far = row_y(2, core)
        for way in range(2):
            arrived(ids[i, 3 + way], gath.at[p, far, tokens(hf, way)])
        src = gath.at[p, far, tokens(hf)]
        ids[i, 7] = push(src, src, sibling)
        if hf == 0:
            own_loads[p].wait()
        for idx, k in ((2, 0), (5, Y - 1), (6, 1), (7, 2)):
            arrived(ids[i, idx], gath.at[p, row_y(k, 1 - core), tokens(hf)])

    direct(0)
    proj_load.wait()
    rim_id = push(proj.at[:, pl.ds(TOK - RIM, RIM), :], rim_in, after)
    direct(1)
    direct(2)
    w_loads = []
    for p in range(PARTS):
        for blk in range(2 * Y):
            copy = pltpu.make_async_copy(
                w_hbm.at[:, pl.ds(512 * blk + LANES * ORDER[p], LANES)],
                wv.at[p, :, pl.ds(LANES * blk, LANES)],
                lsem.at[p * 9 + blk],
            )
            copy.start()
            w_loads.append(copy)

    def widen(b, carry):
        rows = pl.ds(pl.multiple_of(b * LANES, LANES), LANES)
        dest = pl.ds(pl.multiple_of(b * LANES + RIM, RIM), LANES)
        for a in range(3):
            block = proj[a, rows, :].astype(F32)
            for h in range(2):
                projx[a, h, dest, :] = block[:, LANES * h : LANES * h + LANES]
        return carry

    lax.fori_loop(0, BLOCKS, widen, 0)

    def featurize(b):
        start = b * LANES + RIM
        cols = pl.ds(b * LANES if isinstance(b, int) else pl.multiple_of(b * LANES, LANES), LANES)
        for h in range(2):
            chans = pl.ds(LANES * h, LANES)
            turned = []
            for a in range(3):
                total = ff[a, pl.ds(0, 1), chans] * projx[a, h, pl.ds(start, LANES), :]
                for i in range(1, TAPS):
                    total = total + ff[a, pl.ds(i, 1), chans] * projx[a, h, pl.ds(start - i, LANES), :]
                total = total.T
                feat[a, chans, cols] = total
                turned.append(total)
            product = (turned[1] * turned[2]).astype(BF16)
            ahead = b * LANES + LANES
            kvx[chans, pl.ds(ahead if isinstance(b, int) else pl.multiple_of(ahead, LANES), LANES)] = product

    featurize(BLOCKS - 1)
    hist_id = push(kvx.at[:, pl.ds(TOK, LANES)], kvx.at[:, pl.ds(0, LANES)], after)

    def feat_loop(b, carry):
        featurize(b)
        return carry

    lax.fori_loop(1, BLOCKS - 1, feat_loop, 0)
    arrived(rim_id, rim_in)
    for a in range(3):
        before = jnp.where(s == 0, 0.0, rim_in[a].astype(F32))
        for h in range(2):
            projx[a, h, pl.ds(0, RIM), :] = before[:, LANES * h : LANES * h + LANES]
    featurize(0)

    forward(0)
    direct(3)

    arrived(hist_id, kvx.at[:, pl.ds(0, LANES)])
    past = kvx[:, pl.ds(0, LANES)]
    kvx[:, pl.ds(0, LANES)] = jnp.where(s == 0, jnp.zeros_like(past), past)

    def stacked(ref, rows, first, count=BLOCKS):
        return jnp.concatenate(
            [ref[rows, pl.ds(LANES * (b + first), LANES)] for b in range(count)], axis=0
        )

    def convolve(g, carry):
        rows = pl.ds(pl.multiple_of(g * GS, GS), GS)
        windows = jnp.concatenate([stacked(kvx, rows, 0), stacked(kvx, rows, 1)], axis=1)
        result = dot(windows, toep[g], NN)
        for b in range(BLOCKS):
            cols = pl.ds(LANES * b, LANES)
            piece = result[GS * b : GS * b + GS]
            conv[rows, cols] = piece
            mix[q, rows, cols] = (feat[0, rows, cols] * piece).astype(BF16)
        return carry

    mix_ids = []
    for h in range(2):
        lax.fori_loop(h * GROUPS // 2, (h + 1) * GROUPS // 2, convolve, 0, unroll=UNROLL)
        chans = pl.ds(LANES * h, LANES)
        mix_ids.append((push(mix.at[q, chans], mix.at[q, chans], column), chans))

    rs = {}
    top, bottom = pl.ds(0, CH // 2), pl.ds(CH // 2, CH // 2)

    def side(n):
        return q if n % 2 == 0 else 1 - q

    def partial_weight(n):
        p, hh = n // 2, side(n)

        def pair(i, carry):
            rhs = jnp.concatenate([gath[p, 2 * i], gath[p, 2 * i + 1]], axis=1)
            result = dot(mix[hh], rhs, NN).astype(BF16)
            part[n, 2 * i] = result[:, :LANES]
            part[n, 2 * i + 1] = result[:, LANES:]
            return carry

        lax.fori_loop(0, Y, pair, 0)

    def hop(n, k):
        ahead, back = (z + k) % Z, (z - k + Z) % Z
        if k == 4:
            rs[n, 0, 0] = push(part.at[n, ahead, top], rsbuf.at[n, 0, 0, top], at_z(1))
            rs[n, 1, 0] = push(part.at[n, ahead, bottom], rsbuf.at[n, 1, 0, bottom], at_z(Z - 1))
            return
        step = 3 - k
        for way, dest, span, there in ((0, ahead, top, 1), (1, back, bottom, Z - 1)):
            rows = span if k == 3 else pl.ds(0, CH)
            arrived(rs[n, way, step], rsbuf.at[n, way, step, rows])
            part[n, dest, rows] = (
                part[n, dest, rows].astype(F32) + rsbuf[n, way, step, rows].astype(F32)
            ).astype(BF16)
            rs[n, way, step + 1] = push(part.at[n, dest], rsbuf.at[n, way, step + 1], at_z(there))

    def final_sum(n):
        for way in range(2):
            arrived(rs[n, way, 3], rsbuf.at[n, way, 3])
        gwacc[n // 2, side(n)] = (
            part[n, z].astype(F32) + rsbuf[n, 0, 3].astype(F32) + rsbuf[n, 1, 3].astype(F32)
        )

    xids = []

    def exchange(pair):
        xs[pair] = gwacc[2 * pair + 1 - xh].astype(BF16)
        xids.append(push(xs.at[pair], xr.at[pair], across))

    def weight(p):
        for n in (2 * p, 2 * p + 1):
            partial_weight(n)
            hop(n, 4)

    def hops(p, k):
        for n in (2 * p, 2 * p + 1):
            hop(n, k)

    def finals(p):
        for n in (2 * p, 2 * p + 1):
            final_sum(n)
        if p % 2 == 1:
            exchange(p // 2)

    def mix_tile(p, hh, j):
        trows = pl.ds(pl.multiple_of(j * CH, CH), CH)
        crows = pl.ds(pl.multiple_of(hh * CH, CH), CH)
        rhs = jnp.concatenate([gath[p, i, trows, :] for i in range(2 * Y)], axis=1)
        return dot(wv[p, crows, :], rhs, NT)

    def partial_mix(i):
        p, hf = PIECES[i]

        def tile(j, carry):
            for hh in range(2):
                value = mix_tile(p, hh, j)
                if p == 0:
                    pm[j, hh] = value
                else:
                    pm[j, hh] += value
            return carry

        lax.fori_loop(2 * hf, 2 * hf + 2, tile, 0)

    gm_ids = {}

    def last_mix(hf):
        for j in (2 * hf, 2 * hf + 1):
            gms[j] = (pm[j, 1 - q] + mix_tile(PARTS - 1, 1 - q, j)).astype(BF16)
            gm_ids[j] = push(gms.at[j], gmr.at[j], column)

    def own_mix(hf):
        for j in (2 * hf, 2 * hf + 1):
            pm[j, q] += mix_tile(PARTS - 1, q, j)

    future = []

    def cotangents(hf):
        for j in (2 * hf, 2 * hf + 1):
            arrived(gm_ids[j], gmr.at[j])
            cols = pl.ds(CH * j, CH)
            cot = (pm[j, q] + gmr[j].astype(F32)).astype(BF16).astype(F32)
            gcx[:, cols] = (cot * feat[0, :, cols]).astype(BF16)
            if j == 0:
                future.append(push(gcx.at[:, pl.ds(0, LANES)], gcx.at[:, pl.ds(TOK, LANES)], behind))
            grad = (cot * conv[:, cols]).astype(BF16).astype(F32)
            for h in range(2):
                gtok[0, h, cols, :] = grad[LANES * h : LANES * h + LANES].T

    lane = lax.broadcasted_iota(jnp.int32, (LANES, LANES), 1)
    row = lax.broadcasted_iota(jnp.int32, (LANES, LANES), 0)

    def lag_sums():
        def lags(g, carry):
            rows = pl.ds(pl.multiple_of(g * GS, GS), GS)
            cot = stacked(gcx, rows, 0)
            windows = jnp.concatenate([stacked(kvx, rows, 0), stacked(kvx, rows, 1)], axis=1)
            both = dot(cot, windows, TN)
            table = jnp.where(lane > row, both[:, :LANES], both[:, LANES:])
            height = LANES // 2
            while height >= 8:
                table = table[:height] + pltpu.roll(table[height:], LANES - height, 1)
                height //= 2
            lagt[pl.ds(pl.multiple_of(g * 8, 8), 8), :] = table
            return carry

        lax.fori_loop(0, GROUPS, lags, 0, unroll=UNROLL)
        table = lagt[...]
        for bit in (1, 2, 4):
            table = jnp.where((sub // bit) % 2 == 1, pltpu.roll(table, LANES - bit, 1), table)
        sums = jnp.sum(table.reshape(GROUPS, 8, LANES), axis=1)
        turned = ((lane + row) % LANES == 0).astype(F32)
        sums = lax.dot_general(
            sums, turned, NN, precision=lax.Precision.HIGHEST, preferred_element_type=F32
        )
        for c in range(4):
            red[c, pl.ds(0, 4), :] = sums[4 * c : 4 * c + 4]

    def deconvolve(first, count):
        def group(g, carry):
            rows = pl.ds(pl.multiple_of(g * GS, GS), GS)
            windows = jnp.concatenate(
                [stacked(gcx, rows, first, count), stacked(gcx, rows, first + 1, count)], axis=1
            )
            band = jnp.concatenate(
                [toep[g, pl.ds(LANES, LANES), :], toep[g, pl.ds(0, LANES), :]], axis=1
            )
            result = dot(windows, band, NT)
            for b in range(count):
                cols = pl.ds(LANES * (first + b), LANES)
                piece = result[GS * b : GS * b + GS]
                gback[0, rows, cols] = (piece * feat[2, rows, cols]).astype(BF16).astype(F32)
                gback[1, rows, cols] = (piece * feat[1, rows, cols]).astype(BF16).astype(F32)
            return carry

        lax.fori_loop(0, GROUPS, group, 0, unroll=UNROLL)

        def turn(b, carry):
            cols = pl.ds(pl.multiple_of(b * LANES, LANES), LANES)
            for a in range(2):
                for h in range(2):
                    gtok[a + 1, h, cols, :] = gback[a, pl.ds(LANES * h, LANES), cols].T
            return carry

        lax.fori_loop(first, first + count, turn, 0)

    red[...] = jnp.zeros_like(red)
    for copy in w_loads:
        copy.wait()
    forward(1)
    direct(4)
    finish(0)
    partial_mix(0)
    forward(2)
    direct(5)
    finish(1)
    partial_mix(1)
    forward(3)
    direct(6)
    for idx, chans in mix_ids:
        arrived(idx, mix.at[1 - q, chans])
    weight(0)
    finish(2)
    partial_mix(2)
    forward(4)
    direct(7)
    hops(0, 3)
    finish(3)
    partial_mix(3)
    forward(5)
    weight(1)
    hops(0, 2)
    finish(4)
    partial_mix(4)
    forward(6)
    hops(1, 3)
    finish(5)
    last_mix(0)
    own_mix(0)
    forward(7)
    hops(0, 1)
    finish(6)
    partial_mix(6)
    weight(2)
    hops(1, 2)
    finish(7)
    last_mix(1)
    weight(3)
    own_mix(1)
    cotangents(0)
    hops(2, 3)
    finals(0)
    hops(1, 1)
    early = 3
    deconvolve(0, early)
    for a in range(3):
        for h in range(2):
            rim_out[a, :, pl.ds(LANES * h, LANES)] = gtok[a, h, pl.ds(0, RIM), :].astype(BF16)
    back_id = push(rim_out, rim_back, behind)
    hops(3, 3)
    hops(2, 2)
    finals(1)
    hops(3, 2)
    cotangents(1)
    hops(2, 1)
    lag_sums()
    arrived(future[0], gcx.at[:, pl.ds(TOK, LANES)])
    coming = gcx[:, pl.ds(TOK, LANES)]
    gcx[:, pl.ds(TOK, LANES)] = jnp.where(s == seqs - 1, jnp.zeros_like(coming), coming)
    hops(3, 1)
    deconvolve(early, BLOCKS - early)

    span = 64

    def tap_sums(a, h):
        def body(b, sums):
            start = pl.multiple_of(b * span, span)
            grad = gtok[a, h, pl.ds(start, span), :]
            out = []
            for i in range(TAPS):
                value = grad * projx[a, h, pl.ds(start + RIM - i, span), :]
                out.append(sums[i] + jnp.sum(value.reshape(span // 8, 8, LANES), axis=0))
            return tuple(out)

        sums = lax.fori_loop(0, TOK // span, body, tuple(jnp.zeros((8, LANES), F32) for _ in range(TAPS)))
        for i in range(TAPS):
            at = 4 + 2 * (2 * a + h) + i // 4
            red[at, pl.ds(i % 4, 1), :] = jnp.sum(sums[i], axis=0, keepdims=True)

    for a in range(3):
        for h in range(2):
            tap_sums(a, h)
    red_ids = [push(red.at[(s + k) % seqs], redr.at[k], at_s(k)) for k in range(1, seqs)]

    def taps_back(a, h, first, count):
        chans = pl.ds(LANES * h, LANES)

        def body(b, carry):
            start = pl.multiple_of(b * span, span)
            total = ff[a, pl.ds(0, 1), chans] * gtok[a, h, pl.ds(start, span), :]
            for i in range(1, TAPS):
                total = total + ff[a, pl.ds(i, 1), chans] * gtok[a, h, pl.ds(start + i, span), :]
            gp_out[a, pl.ds(start, span), chans] = total.astype(BF16)
            return carry

        lax.fori_loop(first, first + count, body, 0)

    finals(2)
    for h in range(2):
        taps_back(0, h, 0, TOK // span - 1)
    finals(3)
    total = red[s]
    for k in range(1, seqs):
        arrived(red_ids[k - 1], redr.at[k])
        total = total + redr[k]
    redt[...] = total * grad_scale
    redo[s] = redt[...]
    all_ids = [push(redt, redo.at[s], at_s(k)) for k in range(1, seqs)]
    for a in (1, 2):
        for h in range(2):
            taps_back(a, h, 0, TOK // span - 1)
    arrived(back_id, rim_back)
    for a in range(3):
        rest = jnp.where(s == seqs - 1, 0.0, rim_back[a].astype(F32))
        for h in range(2):
            gtok[a, h, pl.ds(TOK, RIM), :] = rest[:, LANES * h : LANES * h + LANES]
            taps_back(a, h, TOK // span - 1, 1)

    for pair in range(2):
        arrived(xids[pair], xr.at[pair])
        for hh in range(2):
            gw_out[pl.ds(CH * hh, CH), pl.ds(LANES * pair, LANES)] = (
                gwacc[2 * pair + xh, hh] + xr[pair, hh].astype(F32)
            ) * grad_scale

    for k in range(1, seqs):
        arrived(all_ids[k - 1], redo.at[(s + seqs - k) % seqs])
    for c in range(4):
        gl_out[pl.ds(4 * c, 4), :] = redo[c, pl.ds(0, 4), :]
    for a in range(3):
        for h in range(2):
            at = 4 + 2 * (2 * a + h)
            gf_out[a, pl.ds(0, 4), pl.ds(LANES * h, LANES)] = redo[at, pl.ds(0, 4), :]
            gf_out[a, pl.ds(4, 3), pl.ds(LANES * h, LANES)] = redo[at + 1, pl.ds(0, 3), :]
    for copy in sent:
        copy.wait_send()


def on_device(projections, feat_filters, long_filters, out_weight, grad_output):
    grad_scale = 1.0 / math.sqrt(TOK * 2 * Z)
    vmem = pl.BlockSpec(memory_space=pltpu.VMEM)
    anywhere = pl.BlockSpec(memory_space=pl.ANY)
    return pl.pallas_call(
        functools.partial(kernel, grad_scale),
        out_shape=(
            pltpu.VMEM((3, TOK, CH), BF16),
            pltpu.VMEM((2 * CH, 2 * LANES), F32),
            pltpu.VMEM((GROUPS, LANES), F32),
            pltpu.VMEM((3, TAPS, CH), F32),
        ),
        in_specs=[anywhere, vmem, vmem, anywhere, anywhere],
        out_specs=(vmem, vmem, vmem, vmem),
        scratch_shapes=[
            pltpu.VMEM((3, TOK, CH), BF16),
            pltpu.VMEM((3, 2, TOK + RIM, LANES), F32),
            pltpu.VMEM((3, CH, TOK), F32),
            pltpu.VMEM((CH, TOK + LANES), BF16),
            pltpu.VMEM((CH, TOK), F32),
            pltpu.VMEM((2, CH, TOK), BF16),
            pltpu.VMEM((GROUPS, 2 * LANES, LANES), BF16),
            pltpu.VMEM((PARTS, 2 * CH, 2 * Y * LANES), BF16),
            pltpu.VMEM((PARTS, 2 * Y, TOK, LANES), BF16),
            pltpu.VMEM((TOK // CH, 2, CH, CH), F32),
            pltpu.VMEM((UNITS, Z, CH, LANES), BF16),
            pltpu.VMEM((UNITS, 2, 4, CH, LANES), BF16),
            pltpu.VMEM((PARTS, 2, CH, LANES), F32),
            pltpu.VMEM((2, 2, CH, LANES), BF16),
            pltpu.VMEM((2, 2, CH, LANES), BF16),
            pltpu.VMEM((TOK // CH, CH, CH), BF16),
            pltpu.VMEM((TOK // CH, CH, CH), BF16),
            pltpu.VMEM((CH, TOK + LANES), BF16),
            pltpu.VMEM((2, CH, TOK), F32),
            pltpu.VMEM((3, 2, TOK + RIM, LANES), F32),
            pltpu.VMEM((3, RIM, CH), BF16),
            pltpu.VMEM((3, RIM, CH), BF16),
            pltpu.VMEM((3, RIM, CH), BF16),
            pltpu.VMEM((8 * GROUPS, LANES), F32),
            pltpu.VMEM((2 * Z, 8, LANES), F32),
            pltpu.VMEM((2 * Z, 8, LANES), F32),
            pltpu.VMEM((8, LANES), F32),
            pltpu.VMEM((2 * Z, 8, LANES), F32),
            pltpu.SemaphoreType.DMA((COPIES,)),
            pltpu.SemaphoreType.DMA((COPIES,)),
            pltpu.SemaphoreType.DMA((9 * PARTS + 1,)),
        ],
        compiler_params=pltpu.CompilerParams(
            collective_id=0, has_side_effects=True, vmem_limit_bytes=56 * 1024 * 1024
        ),
        cost_estimate=pl.CostEstimate(
            flops=9_000_000_000, bytes_accessed=20_000_000, transcendentals=0
        ),
    )(projections, feat_filters, long_filters, out_weight, grad_output)


def solution(mesh):
    return jax.shard_map(
        on_device,
        mesh=mesh,
        in_specs=(
            P(None, "seq", ("row", "col")),
            P(None, None, ("row", "col")),
            P(("row", "col"), None),
            P("row", "col"),
            P("seq", ("col", "row")),
        ),
        out_specs=(
            P(None, "seq", ("row", "col")),
            P("row", ("col", "seq")),
            P(("row", "col"), None),
            P(None, None, ("row", "col")),
        ),
        check_vma=False,
    )
```

```python
import functools
import math

import jax
import jax.numpy as jnp
from jax import lax
from jax.experimental import pallas as pl
from jax.experimental.pallas import tpu as pltpu
from jax.sharding import PartitionSpec as P

MESH = pl.DeviceIdType.MESH
F32 = jnp.float32
BF16 = jnp.bfloat16
NN = (((1,), (0,)), ((), ()))
NT = (((1,), (1,)), ((), ()))
TN = (((0,), (0,)), ((), ()))
Z = 8
Y = 4
TOK = 1024
CH = 256
LANES = 128
BLOCKS = TOK // LANES
GROUPS = 16
GS = 16
TAPS = 7
PARTS = 4
RIM = 16
ORDER = (0, 2, 1, 3)
UNITS = 2 * PARTS
COPIES = 176
PIECES = ((0, 0), (0, 1), (1, 0), (1, 1), (2, 0), (3, 0), (2, 1), (3, 1))
HALF = TOK // 2
UNROLL = 4


def dot(a, b, dims):
    return lax.dot_general(a, b, dims, preferred_element_type=F32)


def kernel(
    grad_scale,
    proj_hbm,
    ff,
    lf,
    w_hbm,
    go_hbm,
    gp_out,
    gw_out,
    gl_out,
    gf_out,
    proj,
    projx,
    feat,
    kvx,
    conv,
    mix,
    toep,
    wv,
    gath,
    pm,
    part,
    rsbuf,
    gwacc,
    xs,
    xr,
    gms,
    gmr,
    gcx,
    gback,
    gtok,
    rim_in,
    rim_out,
    rim_back,
    lagt,
    red,
    redr,
    redt,
    redo,
    ssem,
    rsem,
    lsem,
):
    s = lax.axis_index("seq")
    r = lax.axis_index("row")
    q = lax.axis_index("col")
    seqs = 2 * Z
    z, xh = s // 2, s % 2
    y, core = r // 2, r % 2

    def at_z(k):
        return (((z + k) % Z) * 2 + xh, r, q)

    def at_s(k):
        return ((s + k) % seqs, r, q)

    def at_y(k):
        return (s, ((y + k) % Y) * 2 + core, q)

    def row_y(k, c):
        return ((y + k) % Y) * 2 + c

    sibling = (s, y * 2 + 1 - core, q)
    across = (z * 2 + 1 - xh, r, q)
    column = (s, r, 1 - q)
    after = ((s + 1) % seqs, r, q)
    behind = ((s + seqs - 1) % seqs, r, q)

    used = [0]
    sent = []

    def push(src, dst, device):
        idx = used[0]
        used[0] += 1
        copy = pltpu.make_async_remote_copy(
            src_ref=src,
            dst_ref=dst,
            send_sem=ssem.at[idx],
            recv_sem=rsem.at[idx],
            device_id=device,
            device_id_type=MESH,
        )
        copy.start()
        sent.append(copy)
        return idx

    def arrived(idx, ref):
        pltpu.make_async_remote_copy(
            src_ref=ref,
            dst_ref=ref,
            send_sem=ssem.at[idx],
            recv_sem=rsem.at[idx],
            device_id=sibling,
            device_id_type=MESH,
        ).wait_recv()

    barrier = pltpu.get_barrier_semaphore()
    partners = [at_s(k) for k in range(1, seqs)] + [at_y(1), at_y(Y - 1), sibling, column]
    for device in partners:
        pl.semaphore_signal(barrier, inc=1, device_id=device, device_id_type=MESH)
    proj_load = pltpu.make_async_copy(proj_hbm, proj, lsem.at[9 * PARTS])
    proj_load.start()
    own_loads = []
    for p in range(PARTS):
        copy = pltpu.make_async_copy(
            go_hbm.at[:, pl.ds(LANES * ORDER[p], LANES)], gath.at[p, r], lsem.at[p * 9 + 8]
        )
        copy.start()
        own_loads.append(copy)

    taps32 = lf[...].astype(F32)
    base = jnp.broadcast_to(taps32[:, None, :], (GROUPS, 8, LANES)).reshape(GROUPS * 8, LANES)
    sub = lax.broadcasted_iota(jnp.int32, (GROUPS * 8, LANES), 0) % 8
    for bit in (1, 2, 4):
        base = jnp.where((sub // bit) % 2 == 1, pltpu.roll(base, bit, 1), base)
    lane3 = lax.broadcasted_iota(jnp.int32, (GROUPS, 16, LANES), 2)
    sub3 = lax.broadcasted_iota(jnp.int32, (GROUPS, 16, LANES), 1)
    for a in range(LANES // 16):
        low = pltpu.roll(base, 16 * a, 1) if a else base
        high = pltpu.roll(base, 16 * a + 8, 1)
        both = jnp.concatenate(
            [low.reshape(GROUPS, 8, LANES), high.reshape(GROUPS, 8, LANES)], axis=1
        )
        later = lane3 < sub3 + 16 * a
        toep[:, pl.ds(16 * a, 16), :] = jnp.where(later, both, 0.0).astype(BF16)
        toep[:, pl.ds(LANES + 16 * a, 16), :] = jnp.where(later, 0.0, both).astype(BF16)

    pl.semaphore_wait(barrier, len(partners))

    ids = {}

    def tokens(hf, quarter=None):
        if quarter is None:
            return pl.ds(HALF * hf, HALF)
        return pl.ds(HALF * hf + HALF // 2 * quarter, HALF // 2)

    def direct(i):
        p, hf = PIECES[i]
        src = go_hbm.at[tokens(hf), pl.ds(LANES * ORDER[p], LANES)]
        dst = gath.at[p, r, tokens(hf)]
        ids[i, 0] = push(src, dst, at_y(1))
        ids[i, 1] = push(src, dst, at_y(Y - 1))
        ids[i, 2] = push(src, dst, sibling)

    def forward(i):
        p, hf = PIECES[i]
        for way, k, there in ((0, Y - 1, 1), (1, 1, Y - 1)):
            slot = row_y(k, core)
            arrived(ids[i, way], gath.at[p, slot, tokens(hf)])
            src = gath.at[p, slot, tokens(hf, way)]
            ids[i, 3 + way] = push(src, src, at_y(there))
            src = gath.at[p, slot, tokens(hf)]
            ids[i, 5 + way] = push(src, src, sibling)

    def finish(i):
        p, hf = PIECES[i]
        far = row_y(2, core)
        for way in range(2):
            arrived(ids[i, 3 + way], gath.at[p, far, tokens(hf, way)])
        src = gath.at[p, far, tokens(hf)]
        ids[i, 7] = push(src, src, sibling)
        if hf == 0:
            own_loads[p].wait()
        for idx, k in ((2, 0), (5, Y - 1), (6, 1), (7, 2)):
            arrived(ids[i, idx], gath.at[p, row_y(k, 1 - core), tokens(hf)])

    direct(0)
    proj_load.wait()
    rim_id = push(proj.at[:, pl.ds(TOK - RIM, RIM), :], rim_in, after)
    direct(1)
    w_loads = []
    for p in range(PARTS):
        for blk in range(2 * Y):
            copy = pltpu.make_async_copy(
                w_hbm.at[:, pl.ds(512 * blk + LANES * ORDER[p], LANES)],
                wv.at[p, :, pl.ds(LANES * blk, LANES)],
                lsem.at[p * 9 + blk],
            )
            copy.start()
            w_loads.append(copy)

    def widen(b, carry):
        rows = pl.ds(pl.multiple_of(b * LANES, LANES), LANES)
        dest = pl.ds(pl.multiple_of(b * LANES + RIM, RIM), LANES)
        for a in range(3):
            block = proj[a, rows, :].astype(F32)
            for h in range(2):
                projx[a, h, dest, :] = block[:, LANES * h : LANES * h + LANES]
        return carry

    lax.fori_loop(0, BLOCKS, widen, 0)

    def featurize(b):
        start = b * LANES + RIM
        cols = pl.ds(b * LANES if isinstance(b, int) else pl.multiple_of(b * LANES, LANES), LANES)
        for h in range(2):
            chans = pl.ds(LANES * h, LANES)
            turned = []
            for a in range(3):
                total = ff[a, pl.ds(0, 1), chans] * projx[a, h, pl.ds(start, LANES), :]
                for i in range(1, TAPS):
                    total = total + ff[a, pl.ds(i, 1), chans] * projx[a, h, pl.ds(start - i, LANES), :]
                total = total.T
                feat[a, chans, cols] = total
                turned.append(total)
            product = (turned[1] * turned[2]).astype(BF16)
            ahead = b * LANES + LANES
            kvx[chans, pl.ds(ahead if isinstance(b, int) else pl.multiple_of(ahead, LANES), LANES)] = product

    featurize(BLOCKS - 1)
    hist_id = push(kvx.at[:, pl.ds(TOK, LANES)], kvx.at[:, pl.ds(0, LANES)], after)

    def feat_loop(b, carry):
        featurize(b)
        return carry

    lax.fori_loop(1, BLOCKS - 1, feat_loop, 0)
    arrived(rim_id, rim_in)
    for a in range(3):
        before = jnp.where(s == 0, 0.0, rim_in[a].astype(F32))
        for h in range(2):
            projx[a, h, pl.ds(0, RIM), :] = before[:, LANES * h : LANES * h + LANES]
    featurize(0)

    forward(0)
    direct(2)

    arrived(hist_id, kvx.at[:, pl.ds(0, LANES)])
    past = kvx[:, pl.ds(0, LANES)]
    kvx[:, pl.ds(0, LANES)] = jnp.where(s == 0, jnp.zeros_like(past), past)

    def stacked(ref, rows, first, count=BLOCKS):
        return jnp.concatenate(
            [ref[rows, pl.ds(LANES * (b + first), LANES)] for b in range(count)], axis=0
        )

    def convolve(g, carry):
        rows = pl.ds(pl.multiple_of(g * GS, GS), GS)
        windows = jnp.concatenate([stacked(kvx, rows, 0), stacked(kvx, rows, 1)], axis=1)
        result = dot(windows, toep[g], NN)
        for b in range(BLOCKS):
            cols = pl.ds(LANES * b, LANES)
            piece = result[GS * b : GS * b + GS]
            conv[rows, cols] = piece
            mix[q, rows, cols] = (feat[0, rows, cols] * piece).astype(BF16)
        return carry

    mix_ids = []
    for h in range(2):
        lax.fori_loop(h * GROUPS // 2, (h + 1) * GROUPS // 2, convolve, 0, unroll=UNROLL)
        chans = pl.ds(LANES * h, LANES)
        mix_ids.append((push(mix.at[q, chans], mix.at[q, chans], column), chans))

    rs = {}
    top, bottom = pl.ds(0, CH // 2), pl.ds(CH // 2, CH // 2)

    def side(n):
        return q if n % 2 == 0 else 1 - q

    def partial_weight(n):
        p, hh = n // 2, side(n)

        def pair(i, carry):
            rhs = jnp.concatenate([gath[p, 2 * i], gath[p, 2 * i + 1]], axis=1)
            result = dot(mix[hh], rhs, NN).astype(BF16)
            part[n, 2 * i] = result[:, :LANES]
            part[n, 2 * i + 1] = result[:, LANES:]
            return carry

        lax.fori_loop(0, Y, pair, 0)

    def hop(n, k):
        ahead, back = (z + k) % Z, (z - k + Z) % Z
        if k == 4:
            rs[n, 0, 0] = push(part.at[n, ahead, top], rsbuf.at[n, 0, 0, top], at_z(1))
            rs[n, 1, 0] = push(part.at[n, ahead, bottom], rsbuf.at[n, 1, 0, bottom], at_z(Z - 1))
            return
        step = 3 - k
        for way, dest, span, there in ((0, ahead, top, 1), (1, back, bottom, Z - 1)):
            rows = span if k == 3 else pl.ds(0, CH)
            arrived(rs[n, way, step], rsbuf.at[n, way, step, rows])
            part[n, dest, rows] = (
                part[n, dest, rows].astype(F32) + rsbuf[n, way, step, rows].astype(F32)
            ).astype(BF16)
            rs[n, way, step + 1] = push(part.at[n, dest], rsbuf.at[n, way, step + 1], at_z(there))

    def final_sum(n):
        for way in range(2):
            arrived(rs[n, way, 3], rsbuf.at[n, way, 3])
        gwacc[n // 2, side(n)] = (
            part[n, z].astype(F32) + rsbuf[n, 0, 3].astype(F32) + rsbuf[n, 1, 3].astype(F32)
        )

    xids = []

    def exchange(pair):
        xs[pair] = gwacc[2 * pair + 1 - xh].astype(BF16)
        xids.append(push(xs.at[pair], xr.at[pair], across))

    def weight(n):
        partial_weight(n)
        hop(n, 4)

    def hops(p, k):
        for n in (2 * p, 2 * p + 1):
            hop(n, k)

    def finals(p):
        for n in (2 * p, 2 * p + 1):
            final_sum(n)
        if p % 2 == 1:
            exchange(p // 2)

    def mix_tile(p, hh, j):
        trows = pl.ds(pl.multiple_of(j * CH, CH), CH)
        crows = pl.ds(pl.multiple_of(hh * CH, CH), CH)
        rhs = jnp.concatenate([gath[p, i, trows, :] for i in range(2 * Y)], axis=1)
        return dot(wv[p, crows, :], rhs, NT)

    def partial_mix(i):
        p, hf = PIECES[i]

        def tile(j, carry):
            for hh in range(2):
                value = mix_tile(p, hh, j)
                if p == 0:
                    pm[j, hh] = value
                else:
                    pm[j, hh] += value
            return carry

        lax.fori_loop(2 * hf, 2 * hf + 2, tile, 0)

    gm_ids = {}

    def last_mix(hf):
        for j in (2 * hf, 2 * hf + 1):
            gms[j] = (pm[j, 1 - q] + mix_tile(PARTS - 1, 1 - q, j)).astype(BF16)
            gm_ids[j] = push(gms.at[j], gmr.at[j], column)

    def own_mix(hf):
        for j in (2 * hf, 2 * hf + 1):
            pm[j, q] += mix_tile(PARTS - 1, q, j)

    future = []

    def cotangents(hf):
        for j in (2 * hf, 2 * hf + 1):
            arrived(gm_ids[j], gmr.at[j])
            cols = pl.ds(CH * j, CH)
            cot = (pm[j, q] + gmr[j].astype(F32)).astype(BF16).astype(F32)
            gcx[:, cols] = (cot * feat[0, :, cols]).astype(BF16)
            if j == 0:
                future.append(push(gcx.at[:, pl.ds(0, LANES)], gcx.at[:, pl.ds(TOK, LANES)], behind))
            grad = (cot * conv[:, cols]).astype(BF16).astype(F32)
            for h in range(2):
                gtok[0, h, cols, :] = grad[LANES * h : LANES * h + LANES].T

    lane = lax.broadcasted_iota(jnp.int32, (LANES, LANES), 1)
    row = lax.broadcasted_iota(jnp.int32, (LANES, LANES), 0)

    def lag_sums():
        def lags(g, carry):
            rows = pl.ds(pl.multiple_of(g * GS, GS), GS)
            cot = stacked(gcx, rows, 0)
            windows = jnp.concatenate([stacked(kvx, rows, 0), stacked(kvx, rows, 1)], axis=1)
            both = dot(cot, windows, TN)
            table = jnp.where(lane > row, both[:, :LANES], both[:, LANES:])
            height = LANES // 2
            while height >= 8:
                table = table[:height] + pltpu.roll(table[height:], LANES - height, 1)
                height //= 2
            lagt[pl.ds(pl.multiple_of(g * 8, 8), 8), :] = table
            return carry

        lax.fori_loop(0, GROUPS, lags, 0, unroll=UNROLL)
        table = lagt[...]
        for bit in (1, 2, 4):
            table = jnp.where((sub // bit) % 2 == 1, pltpu.roll(table, LANES - bit, 1), table)
        sums = jnp.sum(table.reshape(GROUPS, 8, LANES), axis=1)
        turned = ((lane + row) % LANES == 0).astype(F32)
        sums = lax.dot_general(
            sums, turned, NN, precision=lax.Precision.HIGHEST, preferred_element_type=F32
        )
        for c in range(4):
            red[c, pl.ds(0, 4), :] = sums[4 * c : 4 * c + 4]

    def deconvolve(first, count):
        def group(g, carry):
            rows = pl.ds(pl.multiple_of(g * GS, GS), GS)
            windows = jnp.concatenate(
                [stacked(gcx, rows, first, count), stacked(gcx, rows, first + 1, count)], axis=1
            )
            band = jnp.concatenate(
                [toep[g, pl.ds(LANES, LANES), :], toep[g, pl.ds(0, LANES), :]], axis=1
            )
            result = dot(windows, band, NT)
            for b in range(count):
                cols = pl.ds(LANES * (first + b), LANES)
                piece = result[GS * b : GS * b + GS]
                gback[0, rows, cols] = (piece * feat[2, rows, cols]).astype(BF16).astype(F32)
                gback[1, rows, cols] = (piece * feat[1, rows, cols]).astype(BF16).astype(F32)
            return carry

        lax.fori_loop(0, GROUPS, group, 0, unroll=UNROLL)

        def turn(b, carry):
            cols = pl.ds(pl.multiple_of(b * LANES, LANES), LANES)
            for a in range(2):
                for h in range(2):
                    gtok[a + 1, h, cols, :] = gback[a, pl.ds(LANES * h, LANES), cols].T
            return carry

        lax.fori_loop(first, first + count, turn, 0)

    red[...] = jnp.zeros_like(red)
    for copy in w_loads:
        copy.wait()
    forward(1)
    direct(3)
    finish(0)
    partial_mix(0)
    forward(2)
    direct(4)
    finish(1)
    weight(0)
    partial_mix(1)
    forward(3)
    direct(5)
    for idx, chans in mix_ids:
        arrived(idx, mix.at[1 - q, chans])
    weight(1)
    finish(2)
    partial_mix(2)
    forward(4)
    direct(6)
    hop(0, 3)
    finish(3)
    weight(2)
    hop(1, 3)
    forward(5)
    direct(7)
    weight(3)
    hop(0, 2)
    partial_mix(3)
    finish(4)
    hop(1, 2)
    partial_mix(4)
    forward(6)
    hops(1, 3)
    finish(5)
    last_mix(0)
    own_mix(0)
    forward(7)
    finish(6)
    hops(0, 1)
    hops(1, 2)
    weight(4)
    weight(5)
    partial_mix(6)
    finish(7)
    last_mix(1)
    weight(6)
    weight(7)
    own_mix(1)
    hops(1, 1)
    hops(2, 3)
    finals(0)
    cotangents(0)
    early = 3
    deconvolve(0, early)
    for a in range(3):
        for h in range(2):
            rim_out[a, :, pl.ds(LANES * h, LANES)] = gtok[a, h, pl.ds(0, RIM), :].astype(BF16)
    back_id = push(rim_out, rim_back, behind)
    hops(3, 3)
    hops(2, 2)
    finals(1)
    cotangents(1)
    lag_sums()
    hops(3, 2)
    hops(2, 1)
    arrived(future[0], gcx.at[:, pl.ds(TOK, LANES)])
    coming = gcx[:, pl.ds(TOK, LANES)]
    gcx[:, pl.ds(TOK, LANES)] = jnp.where(s == seqs - 1, jnp.zeros_like(coming), coming)
    deconvolve(early, BLOCKS - early)

    span = 64

    def tap_sums(a, h):
        def body(b, sums):
            start = pl.multiple_of(b * span, span)
            grad = gtok[a, h, pl.ds(start, span), :]
            out = []
            for i in range(TAPS):
                value = grad * projx[a, h, pl.ds(start + RIM - i, span), :]
                out.append(sums[i] + jnp.sum(value.reshape(span // 8, 8, LANES), axis=0))
            return tuple(out)

        sums = lax.fori_loop(0, TOK // span, body, tuple(jnp.zeros((8, LANES), F32) for _ in range(TAPS)))
        for i in range(TAPS):
            at = 4 + 2 * (2 * a + h) + i // 4
            red[at, pl.ds(i % 4, 1), :] = jnp.sum(sums[i], axis=0, keepdims=True)

    for a in range(3):
        for h in range(2):
            tap_sums(a, h)
    red_ids = [push(red.at[(s + k) % seqs], redr.at[k], at_s(k)) for k in range(1, seqs)]

    def taps_back(a, h, first, count):
        chans = pl.ds(LANES * h, LANES)

        def body(b, carry):
            start = pl.multiple_of(b * span, span)
            total = ff[a, pl.ds(0, 1), chans] * gtok[a, h, pl.ds(start, span), :]
            for i in range(1, TAPS):
                total = total + ff[a, pl.ds(i, 1), chans] * gtok[a, h, pl.ds(start + i, span), :]
            gp_out[a, pl.ds(start, span), chans] = total.astype(BF16)
            return carry

        lax.fori_loop(first, first + count, body, 0)

    hops(3, 1)
    finals(2)
    for h in range(2):
        taps_back(0, h, 0, TOK // span - 1)
    total = red[s]
    for k in range(1, seqs):
        arrived(red_ids[k - 1], redr.at[k])
        total = total + redr[k]
    redt[...] = total * grad_scale
    redo[s] = redt[...]
    all_ids = [push(redt, redo.at[s], at_s(k)) for k in range(1, seqs)]
    finals(3)
    for a in (1, 2):
        for h in range(2):
            taps_back(a, h, 0, TOK // span - 1)
    arrived(back_id, rim_back)
    for a in range(3):
        rest = jnp.where(s == seqs - 1, 0.0, rim_back[a].astype(F32))
        for h in range(2):
            gtok[a, h, pl.ds(TOK, RIM), :] = rest[:, LANES * h : LANES * h + LANES]
            taps_back(a, h, TOK // span - 1, 1)

    for pair in range(2):
        arrived(xids[pair], xr.at[pair])
        for hh in range(2):
            gw_out[pl.ds(CH * hh, CH), pl.ds(LANES * pair, LANES)] = (
                gwacc[2 * pair + xh, hh] + xr[pair, hh].astype(F32)
            ) * grad_scale

    for k in range(1, seqs):
        arrived(all_ids[k - 1], redo.at[(s + seqs - k) % seqs])
    for c in range(4):
        gl_out[pl.ds(4 * c, 4), :] = redo[c, pl.ds(0, 4), :]
    for a in range(3):
        for h in range(2):
            at = 4 + 2 * (2 * a + h)
            gf_out[a, pl.ds(0, 4), pl.ds(LANES * h, LANES)] = redo[at, pl.ds(0, 4), :]
            gf_out[a, pl.ds(4, 3), pl.ds(LANES * h, LANES)] = redo[at + 1, pl.ds(0, 3), :]
    for copy in sent:
        copy.wait_send()


def on_device(projections, feat_filters, long_filters, out_weight, grad_output):
    grad_scale = 1.0 / math.sqrt(TOK * 2 * Z)
    vmem = pl.BlockSpec(memory_space=pltpu.VMEM)
    anywhere = pl.BlockSpec(memory_space=pl.ANY)
    return pl.pallas_call(
        functools.partial(kernel, grad_scale),
        out_shape=(
            pltpu.VMEM((3, TOK, CH), BF16),
            pltpu.VMEM((2 * CH, 2 * LANES), F32),
            pltpu.VMEM((GROUPS, LANES), F32),
            pltpu.VMEM((3, TAPS, CH), F32),
        ),
        in_specs=[anywhere, vmem, vmem, anywhere, anywhere],
        out_specs=(vmem, vmem, vmem, vmem),
        scratch_shapes=[
            pltpu.VMEM((3, TOK, CH), BF16),
            pltpu.VMEM((3, 2, TOK + RIM, LANES), F32),
            pltpu.VMEM((3, CH, TOK), F32),
            pltpu.VMEM((CH, TOK + LANES), BF16),
            pltpu.VMEM((CH, TOK), F32),
            pltpu.VMEM((2, CH, TOK), BF16),
            pltpu.VMEM((GROUPS, 2 * LANES, LANES), BF16),
            pltpu.VMEM((PARTS, 2 * CH, 2 * Y * LANES), BF16),
            pltpu.VMEM((PARTS, 2 * Y, TOK, LANES), BF16),
            pltpu.VMEM((TOK // CH, 2, CH, CH), F32),
            pltpu.VMEM((UNITS, Z, CH, LANES), BF16),
            pltpu.VMEM((UNITS, 2, 4, CH, LANES), BF16),
            pltpu.VMEM((PARTS, 2, CH, LANES), F32),
            pltpu.VMEM((2, 2, CH, LANES), BF16),
            pltpu.VMEM((2, 2, CH, LANES), BF16),
            pltpu.VMEM((TOK // CH, CH, CH), BF16),
            pltpu.VMEM((TOK // CH, CH, CH), BF16),
            pltpu.VMEM((CH, TOK + LANES), BF16),
            pltpu.VMEM((2, CH, TOK), F32),
            pltpu.VMEM((3, 2, TOK + RIM, LANES), F32),
            pltpu.VMEM((3, RIM, CH), BF16),
            pltpu.VMEM((3, RIM, CH), BF16),
            pltpu.VMEM((3, RIM, CH), BF16),
            pltpu.VMEM((8 * GROUPS, LANES), F32),
            pltpu.VMEM((2 * Z, 8, LANES), F32),
            pltpu.VMEM((2 * Z, 8, LANES), F32),
            pltpu.VMEM((8, LANES), F32),
            pltpu.VMEM((2 * Z, 8, LANES), F32),
            pltpu.SemaphoreType.DMA((COPIES,)),
            pltpu.SemaphoreType.DMA((COPIES,)),
            pltpu.SemaphoreType.DMA((9 * PARTS + 1,)),
        ],
        compiler_params=pltpu.CompilerParams(
            collective_id=0, has_side_effects=True, vmem_limit_bytes=56 * 1024 * 1024
        ),
        cost_estimate=pl.CostEstimate(
            flops=9_000_000_000, bytes_accessed=20_000_000, transcendentals=0
        ),
    )(projections, feat_filters, long_filters, out_weight, grad_output)


def solution(mesh):
    return jax.shard_map(
        on_device,
        mesh=mesh,
        in_specs=(
            P(None, "seq", ("row", "col")),
            P(None, None, ("row", "col")),
            P(("row", "col"), None),
            P("row", "col"),
            P("seq", ("col", "row")),
        ),
        out_specs=(
            P(None, "seq", ("row", "col")),
            P("row", ("col", "seq")),
            P(("row", "col"), None),
            P(None, None, ("row", "col")),
        ),
        check_vma=False,
    )
```

```python
import functools
import math

import jax
import jax.numpy as jnp
from jax import lax
from jax.experimental import pallas as pl
from jax.experimental.pallas import tpu as pltpu
from jax.sharding import PartitionSpec as P

MESH = pl.DeviceIdType.MESH
F32 = jnp.float32
BF16 = jnp.bfloat16
NN = (((1,), (0,)), ((), ()))
NT = (((1,), (1,)), ((), ()))
TN = (((0,), (0,)), ((), ()))
Z = 8
Y = 4
TOK = 1024
CH = 256
LANES = 128
BLOCKS = TOK // LANES
GROUPS = 16
GS = 16
TAPS = 7
PARTS = 4
RIM = 16
ORDER = (0, 2, 1, 3)
UNITS = 2 * PARTS
COPIES = 176
PIECES = ((0, 0), (0, 1), (1, 0), (1, 1), (2, 0), (3, 0), (2, 1), (3, 1))
HALF = TOK // 2
UNROLL = 4


def dot(a, b, dims):
    return lax.dot_general(a, b, dims, preferred_element_type=F32)


def kernel(
    grad_scale,
    proj_hbm,
    ff,
    lf,
    w_hbm,
    go_hbm,
    gp_out,
    gw_out,
    gl_out,
    gf_out,
    proj,
    projx,
    feat,
    kvx,
    conv,
    mix,
    toep,
    wv,
    gath,
    pm,
    part,
    rsbuf,
    gwacc,
    xs,
    xr,
    gms,
    gmr,
    gcx,
    gback,
    gtok,
    rim_in,
    rim_out,
    rim_back,
    lagt,
    red,
    redr,
    redt,
    redo,
    ssem,
    rsem,
    lsem,
):
    s = lax.axis_index("seq")
    r = lax.axis_index("row")
    q = lax.axis_index("col")
    seqs = 2 * Z
    z, xh = s // 2, s % 2
    y, core = r // 2, r % 2

    def at_z(k):
        return (((z + k) % Z) * 2 + xh, r, q)

    def at_s(k):
        return ((s + k) % seqs, r, q)

    def at_y(k):
        return (s, ((y + k) % Y) * 2 + core, q)

    def row_y(k, c):
        return ((y + k) % Y) * 2 + c

    sibling = (s, y * 2 + 1 - core, q)
    across = (z * 2 + 1 - xh, r, q)
    column = (s, r, 1 - q)
    after = ((s + 1) % seqs, r, q)
    behind = ((s + seqs - 1) % seqs, r, q)

    used = [0]
    sent = []

    def push(src, dst, device):
        idx = used[0]
        used[0] += 1
        copy = pltpu.make_async_remote_copy(
            src_ref=src,
            dst_ref=dst,
            send_sem=ssem.at[idx],
            recv_sem=rsem.at[idx],
            device_id=device,
            device_id_type=MESH,
        )
        copy.start()
        sent.append(copy)
        return idx

    def arrived(idx, ref):
        pltpu.make_async_remote_copy(
            src_ref=ref,
            dst_ref=ref,
            send_sem=ssem.at[idx],
            recv_sem=rsem.at[idx],
            device_id=sibling,
            device_id_type=MESH,
        ).wait_recv()

    barrier = pltpu.get_barrier_semaphore()
    partners = [at_s(k) for k in range(1, seqs)] + [at_y(1), at_y(Y - 1), sibling, column]
    for device in partners:
        pl.semaphore_signal(barrier, inc=1, device_id=device, device_id_type=MESH)
    proj_load = pltpu.make_async_copy(proj_hbm, proj, lsem.at[9 * PARTS])
    proj_load.start()
    own_loads = []
    for p in range(PARTS):
        copy = pltpu.make_async_copy(
            go_hbm.at[:, pl.ds(LANES * ORDER[p], LANES)], gath.at[p, r], lsem.at[p * 9 + 8]
        )
        copy.start()
        own_loads.append(copy)

    taps32 = lf[...].astype(F32)
    base = jnp.broadcast_to(taps32[:, None, :], (GROUPS, 8, LANES)).reshape(GROUPS * 8, LANES)
    sub = lax.broadcasted_iota(jnp.int32, (GROUPS * 8, LANES), 0) % 8
    for bit in (1, 2, 4):
        base = jnp.where((sub // bit) % 2 == 1, pltpu.roll(base, bit, 1), base)
    lane3 = lax.broadcasted_iota(jnp.int32, (GROUPS, 16, LANES), 2)
    sub3 = lax.broadcasted_iota(jnp.int32, (GROUPS, 16, LANES), 1)
    for a in range(LANES // 16):
        low = pltpu.roll(base, 16 * a, 1) if a else base
        high = pltpu.roll(base, 16 * a + 8, 1)
        both = jnp.concatenate(
            [low.reshape(GROUPS, 8, LANES), high.reshape(GROUPS, 8, LANES)], axis=1
        )
        later = lane3 < sub3 + 16 * a
        toep[:, pl.ds(16 * a, 16), :] = jnp.where(later, both, 0.0).astype(BF16)
        toep[:, pl.ds(LANES + 16 * a, 16), :] = jnp.where(later, 0.0, both).astype(BF16)

    pl.semaphore_wait(barrier, len(partners))

    ids = {}

    def tokens(hf, quarter=None):
        if quarter is None:
            return pl.ds(HALF * hf, HALF)
        return pl.ds(HALF * hf + HALF // 2 * quarter, HALF // 2)

    def direct(i):
        p, hf = PIECES[i]
        src = go_hbm.at[tokens(hf), pl.ds(LANES * ORDER[p], LANES)]
        dst = gath.at[p, r, tokens(hf)]
        ids[i, 0] = push(src, dst, at_y(1))
        ids[i, 1] = push(src, dst, at_y(Y - 1))
        ids[i, 2] = push(src, dst, sibling)

    def forward(i):
        p, hf = PIECES[i]
        for way, k, there in ((0, Y - 1, 1), (1, 1, Y - 1)):
            slot = row_y(k, core)
            arrived(ids[i, way], gath.at[p, slot, tokens(hf)])
            src = gath.at[p, slot, tokens(hf, way)]
            ids[i, 3 + way] = push(src, src, at_y(there))
            src = gath.at[p, slot, tokens(hf)]
            ids[i, 5 + way] = push(src, src, sibling)

    def finish(i):
        p, hf = PIECES[i]
        far = row_y(2, core)
        for way in range(2):
            arrived(ids[i, 3 + way], gath.at[p, far, tokens(hf, way)])
        src = gath.at[p, far, tokens(hf)]
        ids[i, 7] = push(src, src, sibling)
        if hf == 0:
            own_loads[p].wait()
        for idx, k in ((2, 0), (5, Y - 1), (6, 1), (7, 2)):
            arrived(ids[i, idx], gath.at[p, row_y(k, 1 - core), tokens(hf)])

    direct(0)
    proj_load.wait()
    rim_id = push(proj.at[:, pl.ds(TOK - RIM, RIM), :], rim_in, after)
    direct(1)
    w_loads = []
    for p in range(PARTS):
        for blk in range(2 * Y):
            copy = pltpu.make_async_copy(
                w_hbm.at[:, pl.ds(512 * blk + LANES * ORDER[p], LANES)],
                wv.at[p, :, pl.ds(LANES * blk, LANES)],
                lsem.at[p * 9 + blk],
            )
            copy.start()
            w_loads.append(copy)

    def widen(b, carry):
        rows = pl.ds(pl.multiple_of(b * LANES, LANES), LANES)
        dest = pl.ds(pl.multiple_of(b * LANES + RIM, RIM), LANES)
        for a in range(3):
            block = proj[a, rows, :].astype(F32)
            for h in range(2):
                projx[a, h, dest, :] = block[:, LANES * h : LANES * h + LANES]
        return carry

    lax.fori_loop(0, BLOCKS, widen, 0)

    def featurize(b):
        start = b * LANES + RIM
        cols = pl.ds(b * LANES if isinstance(b, int) else pl.multiple_of(b * LANES, LANES), LANES)
        for h in range(2):
            chans = pl.ds(LANES * h, LANES)
            turned = []
            for a in range(3):
                total = ff[a, pl.ds(0, 1), chans] * projx[a, h, pl.ds(start, LANES), :]
                for i in range(1, TAPS):
                    total = total + ff[a, pl.ds(i, 1), chans] * projx[a, h, pl.ds(start - i, LANES), :]
                total = total.T
                feat[a, chans, cols] = total
                turned.append(total)
            product = (turned[1] * turned[2]).astype(BF16)
            ahead = b * LANES + LANES
            kvx[chans, pl.ds(ahead if isinstance(b, int) else pl.multiple_of(ahead, LANES), LANES)] = product

    featurize(BLOCKS - 1)
    hist_id = push(kvx.at[:, pl.ds(TOK, LANES)], kvx.at[:, pl.ds(0, LANES)], after)

    def feat_loop(b, carry):
        featurize(b)
        return carry

    lax.fori_loop(1, BLOCKS - 1, feat_loop, 0)
    arrived(rim_id, rim_in)
    for a in range(3):
        before = jnp.where(s == 0, 0.0, rim_in[a].astype(F32))
        for h in range(2):
            projx[a, h, pl.ds(0, RIM), :] = before[:, LANES * h : LANES * h + LANES]
    featurize(0)

    forward(0)
    direct(2)

    arrived(hist_id, kvx.at[:, pl.ds(0, LANES)])
    past = kvx[:, pl.ds(0, LANES)]
    kvx[:, pl.ds(0, LANES)] = jnp.where(s == 0, jnp.zeros_like(past), past)

    def stacked(ref, rows, first, count=BLOCKS):
        return jnp.concatenate(
            [ref[rows, pl.ds(LANES * (b + first), LANES)] for b in range(count)], axis=0
        )

    def convolve(g, carry):
        rows = pl.ds(pl.multiple_of(g * GS, GS), GS)
        windows = jnp.concatenate([stacked(kvx, rows, 0), stacked(kvx, rows, 1)], axis=1)
        result = dot(windows, toep[g], NN)
        for b in range(BLOCKS):
            cols = pl.ds(LANES * b, LANES)
            piece = result[GS * b : GS * b + GS]
            conv[rows, cols] = piece
            mix[q, rows, cols] = (feat[0, rows, cols] * piece).astype(BF16)
        return carry

    mix_ids = []
    for h in range(2):
        lax.fori_loop(h * GROUPS // 2, (h + 1) * GROUPS // 2, convolve, 0, unroll=UNROLL)
        chans = pl.ds(LANES * h, LANES)
        mix_ids.append((push(mix.at[q, chans], mix.at[q, chans], column), chans))

    rs = {}
    top, bottom = pl.ds(0, CH // 2), pl.ds(CH // 2, CH // 2)

    def side(n):
        return q if n % 2 == 0 else 1 - q

    def partial_weight(n):
        p, hh = n // 2, side(n)

        def pair(i, carry):
            rhs = jnp.concatenate([gath[p, 2 * i], gath[p, 2 * i + 1]], axis=1)
            result = dot(mix[hh], rhs, NN).astype(BF16)
            part[n, 2 * i] = result[:, :LANES]
            part[n, 2 * i + 1] = result[:, LANES:]
            return carry

        lax.fori_loop(0, Y, pair, 0)

    def hop(n, k):
        ahead, back = (z + k) % Z, (z - k + Z) % Z
        if k == 4:
            rs[n, 0, 0] = push(part.at[n, ahead, top], rsbuf.at[n, 0, 0, top], at_z(1))
            rs[n, 1, 0] = push(part.at[n, ahead, bottom], rsbuf.at[n, 1, 0, bottom], at_z(Z - 1))
            return
        step = 3 - k
        for way, dest, span, there in ((0, ahead, top, 1), (1, back, bottom, Z - 1)):
            rows = span if k == 3 else pl.ds(0, CH)
            arrived(rs[n, way, step], rsbuf.at[n, way, step, rows])
            part[n, dest, rows] = (
                part[n, dest, rows].astype(F32) + rsbuf[n, way, step, rows].astype(F32)
            ).astype(BF16)
            rs[n, way, step + 1] = push(part.at[n, dest], rsbuf.at[n, way, step + 1], at_z(there))

    def final_sum(n):
        for way in range(2):
            arrived(rs[n, way, 3], rsbuf.at[n, way, 3])
        gwacc[n // 2, side(n)] = (
            part[n, z].astype(F32) + rsbuf[n, 0, 3].astype(F32) + rsbuf[n, 1, 3].astype(F32)
        )

    xids = []

    def exchange(pair):
        xs[pair] = gwacc[2 * pair + 1 - xh].astype(BF16)
        xids.append(push(xs.at[pair], xr.at[pair], across))

    def weight(n):
        partial_weight(n)
        hop(n, 4)

    def hops(p, k):
        for n in (2 * p, 2 * p + 1):
            hop(n, k)

    def finals(p):
        for n in (2 * p, 2 * p + 1):
            final_sum(n)
        if p % 2 == 1:
            exchange(p // 2)

    def mix_tile(p, hh, j):
        trows = pl.ds(pl.multiple_of(j * CH, CH), CH)
        crows = pl.ds(pl.multiple_of(hh * CH, CH), CH)
        rhs = jnp.concatenate([gath[p, i, trows, :] for i in range(2 * Y)], axis=1)
        return dot(wv[p, crows, :], rhs, NT)

    def partial_mix(i):
        p, hf = PIECES[i]

        def tile(j, carry):
            for hh in range(2):
                value = mix_tile(p, hh, j)
                if p == 0:
                    pm[j, hh] = value
                else:
                    pm[j, hh] += value
            return carry

        lax.fori_loop(2 * hf, 2 * hf + 2, tile, 0)

    gm_ids = {}

    def last_mix(hf):
        for j in (2 * hf, 2 * hf + 1):
            gms[j] = (pm[j, 1 - q] + mix_tile(PARTS - 1, 1 - q, j)).astype(BF16)
            gm_ids[j] = push(gms.at[j], gmr.at[j], column)

    def own_mix(hf):
        for j in (2 * hf, 2 * hf + 1):
            pm[j, q] += mix_tile(PARTS - 1, q, j)

    future = []

    def cotangents(hf):
        for j in (2 * hf, 2 * hf + 1):
            arrived(gm_ids[j], gmr.at[j])
            cols = pl.ds(CH * j, CH)
            cot = (pm[j, q] + gmr[j].astype(F32)).astype(BF16).astype(F32)
            gcx[:, cols] = (cot * feat[0, :, cols]).astype(BF16)
            if j == 0:
                future.append(push(gcx.at[:, pl.ds(0, LANES)], gcx.at[:, pl.ds(TOK, LANES)], behind))
            grad = (cot * conv[:, cols]).astype(BF16).astype(F32)
            for h in range(2):
                gtok[0, h, cols, :] = grad[LANES * h : LANES * h + LANES].T

    lane = lax.broadcasted_iota(jnp.int32, (LANES, LANES), 1)
    row = lax.broadcasted_iota(jnp.int32, (LANES, LANES), 0)

    def lag_sums():
        def lags(g, carry):
            rows = pl.ds(pl.multiple_of(g * GS, GS), GS)
            cot = stacked(gcx, rows, 0)
            windows = jnp.concatenate([stacked(kvx, rows, 0), stacked(kvx, rows, 1)], axis=1)
            both = dot(cot, windows, TN)
            table = jnp.where(lane > row, both[:, :LANES], both[:, LANES:])
            height = LANES // 2
            while height >= 8:
                table = table[:height] + pltpu.roll(table[height:], LANES - height, 1)
                height //= 2
            lagt[pl.ds(pl.multiple_of(g * 8, 8), 8), :] = table
            return carry

        lax.fori_loop(0, GROUPS, lags, 0, unroll=UNROLL)
        table = lagt[...]
        for bit in (1, 2, 4):
            table = jnp.where((sub // bit) % 2 == 1, pltpu.roll(table, LANES - bit, 1), table)
        sums = jnp.sum(table.reshape(GROUPS, 8, LANES), axis=1)
        turned = ((lane + row) % LANES == 0).astype(F32)
        sums = lax.dot_general(
            sums, turned, NN, precision=lax.Precision.HIGHEST, preferred_element_type=F32
        )
        for c in range(4):
            red[c, pl.ds(0, 4), :] = sums[4 * c : 4 * c + 4]

    def deconvolve(first, count):
        def group(g, carry):
            rows = pl.ds(pl.multiple_of(g * GS, GS), GS)
            windows = jnp.concatenate(
                [stacked(gcx, rows, first, count), stacked(gcx, rows, first + 1, count)], axis=1
            )
            band = jnp.concatenate(
                [toep[g, pl.ds(LANES, LANES), :], toep[g, pl.ds(0, LANES), :]], axis=1
            )
            result = dot(windows, band, NT)
            for b in range(count):
                cols = pl.ds(LANES * (first + b), LANES)
                piece = result[GS * b : GS * b + GS]
                gback[0, rows, cols] = (piece * feat[2, rows, cols]).astype(BF16).astype(F32)
                gback[1, rows, cols] = (piece * feat[1, rows, cols]).astype(BF16).astype(F32)
            return carry

        lax.fori_loop(0, GROUPS, group, 0, unroll=UNROLL)

        def turn(b, carry):
            cols = pl.ds(pl.multiple_of(b * LANES, LANES), LANES)
            for a in range(2):
                for h in range(2):
                    gtok[a + 1, h, cols, :] = gback[a, pl.ds(LANES * h, LANES), cols].T
            return carry

        lax.fori_loop(first, first + count, turn, 0)

    red[...] = jnp.zeros_like(red)
    for copy in w_loads:
        copy.wait()
    forward(1)
    direct(3)
    finish(0)
    partial_mix(0)
    forward(2)
    direct(4)
    finish(1)
    weight(0)
    partial_mix(1)
    forward(3)
    direct(5)
    finish(2)
    partial_mix(2)
    forward(4)
    direct(6)
    hop(0, 3)
    for idx, chans in mix_ids:
        arrived(idx, mix.at[1 - q, chans])
    weight(1)
    finish(3)
    weight(2)
    hop(1, 3)
    forward(5)
    direct(7)
    weight(3)
    hop(0, 2)
    partial_mix(3)
    finish(4)
    hop(1, 2)
    partial_mix(4)
    forward(6)
    hops(1, 3)
    finish(5)
    last_mix(0)
    own_mix(0)
    forward(7)
    finish(6)
    hops(0, 1)
    hops(1, 2)
    weight(4)
    weight(5)
    partial_mix(6)
    finish(7)
    last_mix(1)
    weight(6)
    weight(7)
    own_mix(1)
    hops(1, 1)
    hops(2, 3)
    finals(0)
    cotangents(0)
    early = 3
    deconvolve(0, early)
    for a in range(3):
        for h in range(2):
            rim_out[a, :, pl.ds(LANES * h, LANES)] = gtok[a, h, pl.ds(0, RIM), :].astype(BF16)
    back_id = push(rim_out, rim_back, behind)
    hops(3, 3)
    hops(2, 2)
    finals(1)
    cotangents(1)
    lag_sums()
    hops(3, 2)
    hops(2, 1)
    arrived(future[0], gcx.at[:, pl.ds(TOK, LANES)])
    coming = gcx[:, pl.ds(TOK, LANES)]
    gcx[:, pl.ds(TOK, LANES)] = jnp.where(s == seqs - 1, jnp.zeros_like(coming), coming)
    deconvolve(early, BLOCKS - early)

    span = 64

    def tap_sums(a, h):
        def body(b, sums):
            start = pl.multiple_of(b * span, span)
            grad = gtok[a, h, pl.ds(start, span), :]
            out = []
            for i in range(TAPS):
                value = grad * projx[a, h, pl.ds(start + RIM - i, span), :]
                out.append(sums[i] + jnp.sum(value.reshape(span // 8, 8, LANES), axis=0))
            return tuple(out)

        sums = lax.fori_loop(0, TOK // span, body, tuple(jnp.zeros((8, LANES), F32) for _ in range(TAPS)))
        for i in range(TAPS):
            at = 4 + 2 * (2 * a + h) + i // 4
            red[at, pl.ds(i % 4, 1), :] = jnp.sum(sums[i], axis=0, keepdims=True)

    for a in range(3):
        for h in range(2):
            tap_sums(a, h)
    red_ids = [push(red.at[(s + k) % seqs], redr.at[k], at_s(k)) for k in range(1, seqs)]

    def taps_back(a, h, first, count):
        chans = pl.ds(LANES * h, LANES)

        def body(b, carry):
            start = pl.multiple_of(b * span, span)
            total = ff[a, pl.ds(0, 1), chans] * gtok[a, h, pl.ds(start, span), :]
            for i in range(1, TAPS):
                total = total + ff[a, pl.ds(i, 1), chans] * gtok[a, h, pl.ds(start + i, span), :]
            gp_out[a, pl.ds(start, span), chans] = total.astype(BF16)
            return carry

        lax.fori_loop(first, first + count, body, 0)

    hops(3, 1)
    finals(2)
    for h in range(2):
        taps_back(0, h, 0, TOK // span - 1)
    total = red[s]
    for k in range(1, seqs):
        arrived(red_ids[k - 1], redr.at[k])
        total = total + redr[k]
    redt[...] = total * grad_scale
    redo[s] = redt[...]
    all_ids = [push(redt, redo.at[s], at_s(k)) for k in range(1, seqs)]
    finals(3)
    for a in (1, 2):
        for h in range(2):
            taps_back(a, h, 0, TOK // span - 1)
    arrived(back_id, rim_back)
    for a in range(3):
        rest = jnp.where(s == seqs - 1, 0.0, rim_back[a].astype(F32))
        for h in range(2):
            gtok[a, h, pl.ds(TOK, RIM), :] = rest[:, LANES * h : LANES * h + LANES]
            taps_back(a, h, TOK // span - 1, 1)

    for pair in range(2):
        arrived(xids[pair], xr.at[pair])
        for hh in range(2):
            gw_out[pl.ds(CH * hh, CH), pl.ds(LANES * pair, LANES)] = (
                gwacc[2 * pair + xh, hh] + xr[pair, hh].astype(F32)
            ) * grad_scale

    for k in range(1, seqs):
        arrived(all_ids[k - 1], redo.at[(s + seqs - k) % seqs])
    for c in range(4):
        gl_out[pl.ds(4 * c, 4), :] = redo[c, pl.ds(0, 4), :]
    for a in range(3):
        for h in range(2):
            at = 4 + 2 * (2 * a + h)
            gf_out[a, pl.ds(0, 4), pl.ds(LANES * h, LANES)] = redo[at, pl.ds(0, 4), :]
            gf_out[a, pl.ds(4, 3), pl.ds(LANES * h, LANES)] = redo[at + 1, pl.ds(0, 3), :]
    for copy in sent:
        copy.wait_send()


def on_device(projections, feat_filters, long_filters, out_weight, grad_output):
    grad_scale = 1.0 / math.sqrt(TOK * 2 * Z)
    vmem = pl.BlockSpec(memory_space=pltpu.VMEM)
    anywhere = pl.BlockSpec(memory_space=pl.ANY)
    return pl.pallas_call(
        functools.partial(kernel, grad_scale),
        out_shape=(
            pltpu.VMEM((3, TOK, CH), BF16),
            pltpu.VMEM((2 * CH, 2 * LANES), F32),
            pltpu.VMEM((GROUPS, LANES), F32),
            pltpu.VMEM((3, TAPS, CH), F32),
        ),
        in_specs=[anywhere, vmem, vmem, anywhere, anywhere],
        out_specs=(vmem, vmem, vmem, vmem),
        scratch_shapes=[
            pltpu.VMEM((3, TOK, CH), BF16),
            pltpu.VMEM((3, 2, TOK + RIM, LANES), F32),
            pltpu.VMEM((3, CH, TOK), F32),
            pltpu.VMEM((CH, TOK + LANES), BF16),
            pltpu.VMEM((CH, TOK), F32),
            pltpu.VMEM((2, CH, TOK), BF16),
            pltpu.VMEM((GROUPS, 2 * LANES, LANES), BF16),
            pltpu.VMEM((PARTS, 2 * CH, 2 * Y * LANES), BF16),
            pltpu.VMEM((PARTS, 2 * Y, TOK, LANES), BF16),
            pltpu.VMEM((TOK // CH, 2, CH, CH), F32),
            pltpu.VMEM((UNITS, Z, CH, LANES), BF16),
            pltpu.VMEM((UNITS, 2, 4, CH, LANES), BF16),
            pltpu.VMEM((PARTS, 2, CH, LANES), F32),
            pltpu.VMEM((2, 2, CH, LANES), BF16),
            pltpu.VMEM((2, 2, CH, LANES), BF16),
            pltpu.VMEM((TOK // CH, CH, CH), BF16),
            pltpu.VMEM((TOK // CH, CH, CH), BF16),
            pltpu.VMEM((CH, TOK + LANES), BF16),
            pltpu.VMEM((2, CH, TOK), F32),
            pltpu.VMEM((3, 2, TOK + RIM, LANES), F32),
            pltpu.VMEM((3, RIM, CH), BF16),
            pltpu.VMEM((3, RIM, CH), BF16),
            pltpu.VMEM((3, RIM, CH), BF16),
            pltpu.VMEM((8 * GROUPS, LANES), F32),
            pltpu.VMEM((2 * Z, 8, LANES), F32),
            pltpu.VMEM((2 * Z, 8, LANES), F32),
            pltpu.VMEM((8, LANES), F32),
            pltpu.VMEM((2 * Z, 8, LANES), F32),
            pltpu.SemaphoreType.DMA((COPIES,)),
            pltpu.SemaphoreType.DMA((COPIES,)),
            pltpu.SemaphoreType.DMA((9 * PARTS + 1,)),
        ],
        compiler_params=pltpu.CompilerParams(
            collective_id=0, has_side_effects=True, vmem_limit_bytes=56 * 1024 * 1024
        ),
        cost_estimate=pl.CostEstimate(
            flops=9_000_000_000, bytes_accessed=20_000_000, transcendentals=0
        ),
    )(projections, feat_filters, long_filters, out_weight, grad_output)


def solution(mesh):
    return jax.shard_map(
        on_device,
        mesh=mesh,
        in_specs=(
            P(None, "seq", ("row", "col")),
            P(None, None, ("row", "col")),
            P(("row", "col"), None),
            P("row", "col"),
            P("seq", ("col", "row")),
        ),
        out_specs=(
            P(None, "seq", ("row", "col")),
            P("row", ("col", "seq")),
            P(("row", "col"), None),
            P(None, None, ("row", "col")),
        ),
        check_vma=False,
    )
```
